32 devices in a mesh: weight: 2 (over y), context: 4 (over z), tensor: 4 (over x, core).
Axes of the slice: x: 2, y: 2, z: 4, core: 2. Of those that a mesh axis runs over, the one named last changes fastest.
Arguments:
- tokens: bfloat16 [2048, 768], P(('weight', 'context')), may hold values from -6 to 6
- segments: int32 [2048], P(('weight', 'context')), may hold values from 0 to 4, as said below
- query_key_value_weight: bfloat16 [1, 768, 3, 768], P(None, 'weight', None, 'tensor'), may hold values from -0.3125 to 0.3125
- input_bias: float32 [1, 2, 768], P(None, None, 'tensor'), may hold values from -3 to 3
- output_weight: bfloat16 [1, 768, 768], P(None, 'tensor', 'weight'), may hold values from -0.875 to 0.875
- row_bias: float32 [1, 2, 768], replicated, may hold values from -2 to 2
- norm_gain: float32 [1, 2, 768], replicated, may hold values from 0.5 to 1.5
- norm_bias: float32 [1, 2, 768], replicated, may hold values from -2 to 2
- up_weight: bfloat16 [1, 768, 3072], P(None, 'weight', 'tensor'), may hold values from -0.21875 to 0.21875
- up_bias: float32 [1, 3072], P(None, 'tensor'), may hold values from -3 to 3
- down_weight: bfloat16 [1, 3072, 768], P(None, 'tensor', 'weight'), may hold values from -0.109375 to 0.109375
- cotangent: bfloat16 [2048, 768], P(('weight', 'context')), may hold values from -6 to 6
Outputs:
- layer_output: bfloat16 [2048, 768], P(('weight', 'context'))
- grad_tokens: float32 [2048, 768], P(('weight', 'context'))
- grad_input_weight: float32 [1, 768, 3, 768], P(None, 'weight', None, 'tensor')
- grad_input_bias: float32 [1, 2, 768], P(None, None, 'tensor')
- grad_output_weight: float32 [1, 768, 768], P(None, 'tensor', 'weight')
- grad_row_bias: float32 [1, 2, 768], replicated
- grad_norm_gain: float32 [1, 2, 768], replicated
- grad_norm_bias: float32 [1, 2, 768], replicated
- grad_up_weight: float32 [1, 768, 3072], P(None, 'weight', 'tensor')
- grad_up_bias: float32 [1, 3072], P(None, 'tensor')
- grad_down_weight: float32 [1, 3072, 768], P(None, 'tensor', 'weight')
The draws below stay inside these ranges and needn't reach their ends.
Inputs may be any that keep to these rules, and one draw needn't show every extreme that they name: `segments`: within each pack of 1024 tokens the numbers never fall and each of 0 to 4 occurs; number 2 holds tokens among the first 256 and among the last 256 of the pack. Only tokens of one pack with equal numbers attend to each other.
All inputs are finite; a program needn't handle non-finite values.
Results may differ from the reference program's by a relative error of at most 0.013.
The reference program's roundings to bfloat16 on the way count: a program that leaves them out, or rounds other values in their place, can miss the bound.
Values may be sent and summed in bfloat16 or wider, within the bound.
No kernel may reach another device: no remote copies, remote signals or barrier semaphores. Data moves between devices by JAX's collectives and lax.ppermute only.
A program may use at most 64 MiB of HBM per device.

```python
import jax
import jax.numpy as jnp
from jax import lax

D = 768
H = 12
HD = 64
FF = 3072
LAYERS = 1
TOK_DEV = 256
LENGTH = 1024
TOKENS = 2048
N_WEIGHT = 2


def draw_segments(key, part):
    pack_count = TOKENS // LENGTH
    start_key, finish_key, early_key, late_key = jax.random.split(jax.random.fold_in(key, 11), 4)
    half_block = TOK_DEV // 2
    long_start = jax.random.randint(start_key, (pack_count, 1), 2, half_block)
    long_finish = jax.random.randint(finish_key, (pack_count, 1), LENGTH - half_block, LENGTH - 1)
    early_cut = jax.random.randint(early_key, (pack_count, 1), 1, long_start)
    late_cut = jax.random.randint(late_key, (pack_count, 1), long_finish + 1, LENGTH)
    position = jnp.arange(LENGTH, dtype=jnp.int32)[None, :]
    numbers = (position >= early_cut).astype(jnp.int32) + (position >= long_start).astype(jnp.int32) + (position >= long_finish).astype(jnp.int32) + (position >= late_cut).astype(jnp.int32)
    return numbers.reshape(TOKENS)


def level_of(rng, extent, shards, low, top_value):
    factor_of = 1.0
    for axis_at, parts in shards:
        draws = jax.random.uniform(jax.random.fold_in(jax.random.fold_in(rng, 6), axis_at), (parts,), jnp.float32, low / len(shards), top_value / len(shards))
        factor_of = factor_of * jnp.repeat(jnp.exp(draws), extent[axis_at] // parts).reshape((-1,) + (1,) * (len(extent) - 1 - axis_at))
    return factor_of


def gaussian(own_key, dims, width, reach, pieces=(), kind=jnp.bfloat16):
    factor_of = level_of(own_key, dims, pieces, -0.22, 0.18) if pieces else 1.0
    values = jax.random.normal(own_key, dims, jnp.float32) * width * factor_of
    return jnp.minimum(jnp.maximum(values, -reach), reach).astype(kind)


def setup_inputs(seed: int = 0) -> dict:
    seeds = jax.random.split(jax.random.key(seed), 13)
    tokens = gaussian(seeds[0], (TOKENS, D), 1.0, 6.0, ((0, 8),))
    segments = draw_segments(jax.random.fold_in(seeds[12], 71), 0)
    query_key_value_weight = gaussian(seeds[2], (LAYERS, D, 3, D), (D // 2) ** -0.5, 0.3125, ((1, 2), (3, 4)))
    input_bias = gaussian(seeds[3], (LAYERS, 2, D), 0.5, 3.0, ((2, 4),), jnp.float32)
    output_weight = gaussian(seeds[4], (LAYERS, D, D), (D // 16) ** -0.5, 0.875, ((1, 4), (2, 2)))
    row_bias = gaussian(seeds[5], (LAYERS, 2, D), 0.3, 2.0, (), jnp.float32)
    norm_gain = jnp.clip(1.0 + 0.1 * jax.random.normal(seeds[6], (LAYERS, 2, D), jnp.float32), 0.5, 1.5)
    norm_bias = gaussian(seeds[7], (LAYERS, 2, D), 0.3, 2.0, (), jnp.float32)
    up_weight = gaussian(seeds[8], (LAYERS, D, FF), D ** -0.5, 0.21875, ((1, 2), (2, 4)))
    up_bias = gaussian(seeds[9], (LAYERS, FF), 0.5, 3.0, ((1, 4),), jnp.float32)
    down_weight = gaussian(seeds[10], (LAYERS, FF, D), FF ** -0.5, 0.109375, ((1, 4), (2, 2)))
    cotangent = gaussian(seeds[11], (TOKENS, D), 1.0, 6.0, ((0, 8),))
    return {"tokens": tokens, "segments": segments, "query_key_value_weight": query_key_value_weight, "input_bias": input_bias, "output_weight": output_weight, "row_bias": row_bias, "norm_gain": norm_gain, "norm_bias": norm_bias, "up_weight": up_weight, "up_bias": up_bias, "down_weight": down_weight, "cotangent": cotangent}


EPSILON = 1e-05
NEG_FILL = -1e+30
ROOT_HALF = 0.7071067811865476
MAXIMAL_ACCURACY = lax.Precision.HIGHEST

@jax.custom_vjp
def low(v):
    return lax.optimization_barrier(v.astype(jnp.bfloat16)).astype(jnp.float32)

@jax.custom_vjp
def low_back(v):
    return v

def low_keep(v):
    return (low(v), None)

def low_pass(kept, grad):
    return (grad,)

def back_keep(v):
    return (v, None)

def back_low(kept, grad):
    return (low(grad),)
low.defvjp(low_keep, low_pass)
low_back.defvjp(back_keep, back_low)

def product(left, right):
    return jnp.dot(left, right, precision=MAXIMAL_ACCURACY)

def normalize(summed, gain_vector, shift_vector):
    center = summed - lax.optimization_barrier(jnp.mean(summed, axis=-1, keepdims=True))
    inverse = lax.rsqrt(lax.optimization_barrier(jnp.mean(center * center, axis=-1, keepdims=True)) + EPSILON)
    return center * inverse * gain_vector + shift_vector

def one_layer(hidden_state, pack_segments, query_key_value_weight, input_bias, output_weight, row_bias, norm_gain, norm_bias, up_weight, up_bias, down_weight):
    count_of_rows = hidden_state.shape[0]
    projected_rows = jnp.einsum('nw,wrk->nrk', low(hidden_state), query_key_value_weight, precision=MAXIMAL_ACCURACY)
    queries = low(low_back(projected_rows[:, 0]) + input_bias[0])
    key_rows = low(low_back(projected_rows[:, 1]))
    value_rows = low(low_back(projected_rows[:, 2]) + input_bias[1])
    query_heads = queries.reshape(count_of_rows, H, HD)
    key_heads = key_rows.reshape(count_of_rows, H, HD)
    value_heads = value_rows.reshape(count_of_rows, H, HD)
    scores = jnp.einsum('qhe,khe->hqk', query_heads, key_heads, precision=MAXIMAL_ACCURACY) * HD ** (-0.5)
    same_doc = pack_segments[:, None] == pack_segments[None, :]
    scores = low_back(jnp.where(same_doc[None], scores, NEG_FILL))
    row_max = lax.optimization_barrier(jnp.max(scores, axis=-1, keepdims=True))
    exponent = jnp.exp(scores - row_max)
    probability = low(exponent / lax.optimization_barrier(jnp.sum(exponent, axis=-1, keepdims=True)))
    context = jnp.einsum('hqk,khe->qhe', probability, value_heads, precision=MAXIMAL_ACCURACY)
    context = low(low_back(context.reshape(count_of_rows, H * HD)))
    attended = low_back(product(context, output_weight)) + row_bias[0]
    first_norm = normalize(hidden_state + attended, norm_gain[0], norm_bias[0])
    preactivation = low_back(product(low(first_norm), up_weight)) + up_bias
    activated = low(preactivation * (0.5 * (1.0 + lax.erf(preactivation * ROOT_HALF))))
    feed_output = low_back(product(activated, down_weight)) + row_bias[1]
    return normalize(first_norm + feed_output, norm_gain[1], norm_bias[1])

def reference(tokens, segments, query_key_value_weight, input_bias, output_weight, row_bias, norm_gain, norm_bias, up_weight, up_bias, down_weight, cotangent):
    params = tuple((argument.astype(jnp.float32) for argument in (query_key_value_weight, input_bias, output_weight, row_bias, norm_gain, norm_bias, up_weight, up_bias, down_weight)))
    pack_tokens = tokens.astype(jnp.float32).reshape(N_WEIGHT, LENGTH, D)
    pack_numbers = segments.reshape(N_WEIGHT, LENGTH)
    pack_cots = cotangent.astype(jnp.float32).reshape(N_WEIGHT, LENGTH, D)

    def per_pack(totals, pack_item):
        pack_rows, pack_segments, pack_grad = pack_item

        def forward(inputs, weights):
            hidden_state = inputs
            for layer_index in range(LAYERS):
                hidden_state = one_layer(hidden_state, pack_segments, *[argument[layer_index] for argument in weights])
            return hidden_state
        layer_result, pullback = jax.vjp(forward, pack_rows, params)
        grad_inputs, grad_params = pullback(pack_grad)
        totals = tuple((earlier + later for earlier, later in zip(totals, grad_params)))
        return (totals, (layer_result.astype(jnp.bfloat16), grad_inputs))
    zero_grads = tuple((jnp.zeros_like(argument) for argument in params))
    totals, (outputs, grads_in) = lax.scan(per_pack, zero_grads, (pack_tokens, pack_numbers, pack_cots))
    return (outputs.reshape(TOKENS, D), grads_in.reshape(TOKENS, D), totals[0], totals[1], totals[2], totals[3], totals[4], totals[5], totals[6], totals[7], totals[8])
```

```python
import jax
import jax.numpy as jnp
from jax import lax
from jax.sharding import PartitionSpec as P

HD = 64
EPSILON = 1e-05
NEG_FILL = -1e30
ROOT_HALF = 0.7071067811865476
DENSITY_FACTOR = 0.3989422804014327
BF = jnp.bfloat16
F32 = jnp.float32


def product(left, right):
    return jnp.dot(left, right, preferred_element_type=F32)


def product_left(left, right):
    return lax.dot_general(left, right, (((0,), (0,)), ((), ())), preferred_element_type=F32)


def product_right(left, right):
    return lax.dot_general(left, right, (((1,), (1,)), ((), ())), preferred_element_type=F32)


def normalize(summed):
    center = summed - jnp.mean(summed, axis=-1, keepdims=True)
    inverse = lax.rsqrt(jnp.mean(center * center, axis=-1, keepdims=True) + EPSILON)
    return center * inverse, inverse


def normalize_back(grad_output, normed, inverse, gain_vector):
    scaled = grad_output * gain_vector
    return inverse * (
        scaled
        - jnp.mean(scaled, axis=-1, keepdims=True)
        - normed * jnp.mean(scaled * normed, axis=-1, keepdims=True)
    )


def build(mesh):
    count = dict(mesh.shape)
    paired = count["weight"] == 2

    def flip(value, axis, bit):
        return lax.ppermute(value, axis, [(i, i ^ bit) for i in range(count[axis])])

    def bits(axis):
        bit, found = 1, []
        while bit < count[axis]:
            found.append(bit)
            bit *= 2
        return found

    def shards(
        tokens,
        segments,
        query_key_value_weight,
        input_bias,
        output_weight,
        row_bias,
        norm_gain,
        norm_bias,
        up_weight,
        up_bias,
        down_weight,
        cotangent,
    ):
        weight_at = lax.axis_index("weight")
        context_at = lax.axis_index("context")
        core_at = lax.axis_index("tensor") % 2
        rows, width = tokens.shape
        half = rows // 2
        shard_width = input_bias.shape[2]
        heads = shard_width // HD
        packs = count["context"]

        def columns(value):
            if not paired:
                return value
            middle = value.shape[-1] // 2
            swapped = jnp.concatenate([value[..., middle:], value[..., :middle]], axis=-1)
            return jnp.where(weight_at == 0, value, swapped)

        def own_rows(value):
            middle = value.shape[0] // 2
            swapped = jnp.concatenate([value[middle:], value[:middle]], axis=0)
            return jnp.where(core_at == 0, value, swapped)

        def gather_weight(value, axis):
            if paired:
                return [value, flip(value, "weight", 1)]
            return [lax.all_gather(value, "weight", axis=axis, tiled=True)]

        def contract(value, groups):
            step = width // len(groups)
            total = product(value[:, :step], groups[0])
            for number in range(1, len(groups)):
                total = total + product(
                    value[:, number * step : (number + 1) * step], groups[number]
                )
            return total

        def expand(value, groups):
            parts = [product(value, group) for group in groups]
            return parts[0] if len(parts) == 1 else jnp.concatenate(parts, axis=1)

        def contract_right(value, groups):
            step = width // len(groups)
            total = product_right(value[:, :step], groups[0])
            for number in range(1, len(groups)):
                total = total + product_right(
                    value[:, number * step : (number + 1) * step], groups[number]
                )
            return total

        def expand_right(value, groups):
            parts = [product_right(value, group) for group in groups]
            return parts[0] if len(parts) == 1 else jnp.concatenate(parts, axis=1)

        def row_total(partial):
            mine, theirs = partial[:half], partial[half:].astype(BF)
            total = mine + flip(theirs, "tensor", 1).astype(F32)
            for bit in bits("tensor")[1:]:
                low = total.astype(BF)
                total = low.astype(F32) + flip(low, "tensor", bit).astype(F32)
            return total

        def both_halves(value):
            return jnp.concatenate([value, flip(value, "tensor", 1)], axis=0)

        def take_half(value, which):
            middle = value.shape[0] // 2
            return lax.dynamic_slice_in_dim(value, which * middle, middle, axis=0)

        def context_total(value):
            for bit in bits("context"):
                which = (context_at // bit) % 2
                own, other = take_half(value, which), take_half(value, 1 - which)
                value = own + flip(other.astype(BF), "context", bit).astype(F32)
            value = value.astype(BF)
            for bit in reversed(bits("context")):
                which = (context_at // bit) % 2
                other = flip(value, "context", bit)
                value = jnp.where(
                    which == 0,
                    jnp.concatenate([value, other], axis=0),
                    jnp.concatenate([other, value], axis=0),
                )
            return value.astype(F32)

        def context_blocks(value):
            blocks = [value] + [flip(value, "context", j) for j in range(1, packs)]
            return blocks

        def in_order(blocks):
            placed = []
            for at in range(packs):
                chosen = blocks[0]
                for j in range(1, packs):
                    chosen = jnp.where(context_at == (at ^ j), blocks[j], chosen)
                placed.append(chosen)
            return jnp.concatenate(placed, axis=0)

        projection = query_key_value_weight[0].reshape(-1, 3 * shard_width)
        input_groups = gather_weight(projection, 0)
        output_groups = gather_weight(output_weight[0], 1)
        up_groups = gather_weight(up_weight[0], 0)
        down_groups = gather_weight(down_weight[0], 1)

        gains, shifts, row_pair = columns(norm_gain[0]), columns(norm_bias[0]), columns(row_bias[0])
        low_rows = own_rows(columns(tokens))
        cotangent_rows = own_rows(columns(cotangent))[:half].astype(F32)
        segment_rows = own_rows(segments)

        own_blocks = [low_rows[:half]] + [
            flip(low_rows[:half], "context", j) for j in range(1, packs)
        ]
        blocks = [low_rows] + [both_halves(block) for block in own_blocks[1:]]
        pack_rows = in_order(blocks)
        pack_segments = in_order(context_blocks(segment_rows))

        bias_pair = input_bias[0]
        projected = contract(pack_rows, input_groups)
        pack_queries = (projected[:, :shard_width] + bias_pair[0]).astype(BF)
        pack_keys = projected[:, shard_width : 2 * shard_width].astype(BF)
        pack_values = (projected[:, 2 * shard_width :] + bias_pair[1]).astype(BF)
        length = pack_rows.shape[0]
        key_heads = pack_keys.reshape(length, heads, HD)
        value_heads = pack_values.reshape(length, heads, HD)
        query_heads = lax.dynamic_slice_in_dim(pack_queries, context_at * rows, rows, 0).reshape(
            rows, heads, HD
        )

        scale = HD ** (-0.5)

        def attention_scores(queries, query_segments):
            scores = (
                jnp.einsum("qhe,khe->hqk", queries, key_heads, preferred_element_type=F32) * scale
            )
            same = query_segments[:, None] == pack_segments[None, :]
            return jnp.where(same[None], scores, NEG_FILL)

        scores = attention_scores(query_heads, segment_rows)
        row_max = jnp.max(scores, axis=-1, keepdims=True)
        exponent = jnp.exp(scores - row_max)
        total = jnp.sum(exponent, axis=-1, keepdims=True)
        probability = (exponent / total).astype(BF)
        log_total = (row_max + jnp.log(total))[..., 0]
        context = jnp.einsum("hqk,khe->qhe", probability, value_heads, preferred_element_type=F32)
        context = context.reshape(rows, shard_width).astype(BF)
        pack_log = in_order(context_blocks(log_total.T)).T

        hidden_half = low_rows[:half].astype(F32)
        attended = row_total(expand(context, output_groups)) + row_pair[0]
        normed_one, inverse_one = normalize(hidden_half + attended)
        first_norm = normed_one * gains[0] + shifts[0]
        first_low = both_halves(first_norm.astype(BF))

        preactivation = contract(first_low, up_groups) + up_bias[0]
        cumulative = 0.5 * (1.0 + lax.erf(preactivation * ROOT_HALF))
        activated = (preactivation * cumulative).astype(BF)
        slope = cumulative + preactivation * DENSITY_FACTOR * jnp.exp(
            -0.5 * preactivation * preactivation
        )
        feed = row_total(expand(activated, down_groups)) + row_pair[1]
        normed_two, inverse_two = normalize(first_norm + feed)
        result = (normed_two * gains[1] + shifts[1]).astype(BF)
        layer_output = columns(own_rows(both_halves(result)))

        grad_two = normalize_back(cotangent_rows, normed_two, inverse_two, gains[1])
        grad_two_low = both_halves(grad_two.astype(BF))

        def owner_total(left, right, axis):
            if paired:
                step = width // 2
                if axis == 0:
                    mine = product_left(left[:, :step], right)
                    theirs = product_left(left[:, step:], right)
                else:
                    mine = product_left(left, right[:, :step])
                    theirs = product_left(left, right[:, step:])
                return mine + flip(theirs.astype(BF), "weight", 1).astype(F32)
            return lax.psum_scatter(
                product_left(left, right).astype(BF), "weight", scatter_dimension=axis, tiled=True
            ).astype(F32)

        grad_down = context_total(owner_total(activated, grad_two_low, 1))
        grad_pre = contract_right(grad_two_low, down_groups) * slope
        grad_pre_low = grad_pre.astype(BF)
        grad_first = grad_two + row_total(expand_right(grad_pre_low, up_groups))
        grad_up = context_total(owner_total(first_low, grad_pre_low, 0))
        grad_one = normalize_back(grad_first, normed_one, inverse_one, gains[0])
        grad_one_low = both_halves(grad_one.astype(BF))
        grad_context = contract_right(grad_one_low, output_groups).astype(BF)
        pack_context = in_order(context_blocks(grad_context))
        grad_out = context_total(owner_total(context, grad_one_low, 1))

        all_queries = pack_queries.reshape(length, heads, HD)
        all_context = pack_context.reshape(length, heads, HD)
        probability = jnp.exp(
            attention_scores(all_queries, pack_segments) - pack_log[:, :, None]
        )
        grad_probability = jnp.einsum(
            "qhe,khe->hqk", all_context, value_heads, preferred_element_type=F32
        )
        grad_values = jnp.einsum(
            "hqk,qhe->khe", probability.astype(BF), all_context, preferred_element_type=F32
        ).reshape(length, shard_width)
        row_dot = jnp.sum(probability * grad_probability, axis=-1, keepdims=True)
        grad_scores = (probability * (grad_probability - row_dot)).astype(BF)
        grad_query = (
            jnp.einsum("hqk,khe->qhe", grad_scores, key_heads, preferred_element_type=F32).reshape(
                length, shard_width
            )
            * scale
        )
        grad_keys = (
            jnp.einsum("hqk,qhe->khe", grad_scores, all_queries, preferred_element_type=F32).reshape(
                length, shard_width
            )
            * scale
        )
        pack_projected = jnp.concatenate([grad_query, grad_keys, grad_values], axis=1).astype(BF)
        grad_input = owner_total(pack_rows, pack_projected, 0)
        own_projected = lax.dynamic_slice_in_dim(pack_projected, context_at * rows, rows, 0)
        grad_half = grad_one + row_total(expand_right(own_projected, input_groups))
        grad_tokens = columns(own_rows(both_halves(grad_half)))

        def sums(value):
            return jnp.sum(value, axis=0)

        small = jnp.stack(
            [
                sums(grad_one),
                sums(grad_two),
                sums(grad_first * normed_one),
                sums(cotangent_rows * normed_two),
                sums(grad_first),
                sums(cotangent_rows),
            ]
        )
        small = columns(small)
        small = small + flip(small, "tensor", 1)
        hidden_sum = sums(grad_pre)
        joined = jnp.concatenate([small.reshape(-1), hidden_sum])
        for bit in bits("context"):
            joined = joined + flip(joined, "context", bit)
        joined = weight_total(joined)
        small = joined[: 6 * width].reshape(3, 2, width)
        bias_grads = weight_total(jnp.stack([sums(grad_query), sums(grad_values)]))
        return (
            layer_output,
            grad_tokens,
            grad_input.reshape(1, -1, 3, shard_width),
            bias_grads[None],
            grad_out[None],
            small[0][None],
            small[1][None],
            small[2][None],
            grad_up[None],
            joined[6 * width :][None],
            grad_down[None],
        )

    def weight_total(value):
        if paired:
            return value + flip(value, "weight", 1)
        return lax.psum(value, "weight")

    return shards


def solution(mesh):
    token_rows = P(("weight", "context"), None)
    input_spec = P(None, "weight", None, "tensor")
    out_spec = P(None, "tensor", "weight")
    placed = (
        token_rows,
        P(("weight", "context")),
        input_spec,
        P(None, None, "tensor"),
        out_spec,
        P(),
        P(),
        P(),
        P(None, "weight", "tensor"),
        P(None, "tensor"),
        out_spec,
        token_rows,
    )
    return jax.shard_map(
        build(mesh),
        mesh=mesh,
        in_specs=placed,
        out_specs=(
            token_rows,
            token_rows,
            input_spec,
            P(None, None, "tensor"),
            out_spec,
            P(),
            P(),
            P(),
            P(None, "weight", "tensor"),
            P(None, "tensor"),
            out_spec,
        ),
        check_vma=False,
    )
```

```python
import functools

import jax
import jax.experimental.pallas as pl
import jax.experimental.pallas.tpu as pltpu
import jax.numpy as jnp
from jax import lax
from jax.sharding import PartitionSpec as P

HD = 64
EPSILON = 1e-05
NEG_FILL = -1e30
ROOT_HALF = 0.7071067811865476
DENSITY_FACTOR = 0.3989422804014327
BF = jnp.bfloat16
F32 = jnp.float32


def product(left, right):
    return jnp.dot(left, right, preferred_element_type=F32)


def product_left(left, right):
    return lax.dot_general(left, right, (((0,), (0,)), ((), ())), preferred_element_type=F32)


def product_right(left, right):
    return lax.dot_general(left, right, (((1,), (1,)), ((), ())), preferred_element_type=F32)


def normalize(summed):
    center = summed - jnp.mean(summed, axis=-1, keepdims=True)
    inverse = lax.rsqrt(jnp.mean(center * center, axis=-1, keepdims=True) + EPSILON)
    return center * inverse, inverse


def normalize_back(grad_output, normed, inverse, gain_vector):
    scaled = grad_output * gain_vector
    return inverse * (
        scaled
        - jnp.mean(scaled, axis=-1, keepdims=True)
        - normed * jnp.mean(scaled * normed, axis=-1, keepdims=True)
    )


VMEM = pl.BlockSpec(memory_space=pltpu.VMEM)
FAR = pl.BlockSpec(memory_space=pltpu.HBM)
ANYWHERE = pl.BlockSpec(memory_space=pl.ANY)
PARAMS = pltpu.CompilerParams(vmem_limit_bytes=40 * 1024 * 1024)


def after(value, *others):
    zero = jnp.zeros((), F32)
    for other in others:
        first = lax.slice(other, (0,) * other.ndim, (1,) * other.ndim).reshape(())
        zero = zero + jnp.minimum(jnp.abs(first.astype(F32)), 0.0)
    return value + zero.astype(value.dtype)


def softmax_block(keys, queries, same):
    scores = jnp.where(same, product_right(keys, queries) * HD**-0.5, NEG_FILL)
    exponent = jnp.exp(scores - jnp.max(scores, axis=0, keepdims=True))
    total = jnp.sum(exponent, axis=0, keepdims=True)
    return (exponent * (1.0 / total)).astype(BF)


def as_column(row):
    return jnp.broadcast_to(row, (8, row.shape[1])).T[:, :1]


def block_start(number, rows):
    return pl.multiple_of((lax.axis_index("context") ^ number) * rows, rows)


def front_kernel(heads, packs, paired, *refs):
    blocks, refs = refs[: 2 * packs], refs[2 * packs :]
    groups = 2 if paired else 1
    b_ref, weights, refs = refs[0], refs[1 : 1 + groups], refs[1 + groups :]
    q_ref, k_ref, v_ref, c_ref, x_ref, row_ref = refs
    width = heads * HD
    model = x_ref.shape[1]
    rows = c_ref.shape[0]
    half = rows // 2
    step = model // groups
    for number in range(packs):
        for which in range(2):
            block = blocks[2 * number + which]
            at = pl.multiple_of(block_start(number, rows) + which * half, half)
            if paired:
                first = lax.axis_index("weight") == 0
                left, right = block[:half, :step], block[:half, step:]
                x_ref[pl.ds(at, half), :step] = jnp.where(first, left, right)
                x_ref[pl.ds(at, half), step:] = jnp.where(first, right, left)
            else:
                x_ref[pl.ds(at, half)] = block[:half]
            row_ref[:, pl.ds(at, half)] = block[half : half + 1, :half].astype(F32)
    for number, (out_ref, bias) in enumerate(((q_ref, 0), (k_ref, None), (v_ref, 1))):
        total = None
        for group in range(groups):
            part = product(
                x_ref[:, group * step : (group + 1) * step],
                weights[group][:, number * width : (number + 1) * width],
            )
            total = part if total is None else total + part
        if bias is not None:
            total = total + b_ref[bias : bias + 1]
        out_ref[...] = total.astype(BF)
    at = block_start(0, rows)
    same = as_column(row_ref[...]) == row_ref[:, pl.ds(at, rows)]
    for head in range(heads):
        lanes = slice(head * HD, (head + 1) * HD)
        probability = softmax_block(k_ref[:, lanes], q_ref[pl.ds(at, rows), lanes], same)
        c_ref[:, lanes] = product(v_ref[:, lanes].T, probability).T.astype(BF)


def front(blocks, biases, groups):
    packs = len(blocks) // 2
    rows = 2 * (blocks[0].shape[0] - 16)
    model = blocks[0].shape[1]
    width = biases.shape[1]
    whole = jax.ShapeDtypeStruct((packs * rows, width), BF)
    return pl.pallas_call(
        functools.partial(front_kernel, width // HD, packs, len(groups) == 2),
        out_shape=(
            whole,
            whole,
            whole,
            jax.ShapeDtypeStruct((rows, width), BF),
            jax.ShapeDtypeStruct((packs * rows, model), BF),
            jax.ShapeDtypeStruct((1, packs * rows), F32),
        ),
        in_specs=[VMEM] * (2 * packs + 1 + len(groups)),
        out_specs=(VMEM,) * 6,
        compiler_params=PARAMS,
    )(*blocks, biases, *groups)


def probability_kernel(heads, block, q_ref, k_ref, row_ref, *refs):
    a_hbm, a_ref, copy_sems = refs[-3:]
    count = q_ref.shape[0] // block

    def copy(number):
        at = pl.multiple_of(number * block, block)
        return pltpu.make_async_copy(
            a_ref.at[:, :, pl.ds(at, block)],
            a_hbm.at[:, :, pl.ds(at, block)],
            copy_sems.at[number],
        )

    def body(number, carry):
        at = pl.multiple_of(number * block, block)
        same = as_column(row_ref[...]) == row_ref[:, pl.ds(at, block)]
        for head in range(heads):
            lanes = slice(head * HD, (head + 1) * HD)
            a_ref[head, :, pl.ds(at, block)] = softmax_block(
                k_ref[:, lanes], q_ref[pl.ds(at, block), lanes], same
            )
        copy(number).start()
        return carry

    lax.fori_loop(0, count, body, 0)
    for number in range(count):
        copy(number).wait()


def probabilities(queries, keys, segments, gates):
    length, width = queries.shape
    heads = width // HD
    block = 256
    return pl.pallas_call(
        functools.partial(probability_kernel, heads, block),
        out_shape=jax.ShapeDtypeStruct((heads, length, length), BF),
        in_specs=[VMEM] * 3 + [ANYWHERE] * len(gates),
        out_specs=FAR,
        scratch_shapes=[
            pltpu.VMEM((heads, length, length), BF),
            pltpu.SemaphoreType.DMA((length // block,)),
        ],
        compiler_params=PARAMS,
    )(queries, keys, segments, *gates)


def attention_back_kernel(heads, packs, a_hbm, q_ref, k_ref, v_ref, *refs):
    blocks, (p_ref, b_ref, a_ref, c_ref, copy_sems) = refs[:packs], refs[-5:]
    width = heads * HD
    scale = jnp.asarray(HD**-0.5, BF)
    copies = [
        pltpu.make_async_copy(a_hbm.at[head], a_ref.at[head], copy_sems.at[head])
        for head in range(heads)
    ]
    for copy in copies:
        copy.start()
    for number, block in enumerate(blocks):
        rows = block.shape[0]
        c_ref[pl.ds(block_start(number, rows), rows)] = block[...]
    for head in range(heads):
        lanes = slice(head * HD, (head + 1) * HD)
        grad_context = c_ref[:, lanes]
        copies[head].wait()
        low = a_ref[head]
        wide = low.astype(F32)
        weighted = wide * product_right(v_ref[:, lanes], grad_context)
        row_dot = jnp.sum(weighted, axis=0, keepdims=True)
        grad_scores = (weighted - wide * row_dot).astype(BF)
        grad_values = product(low, grad_context)
        grad_keys = product(grad_scores, q_ref[:, lanes] * scale)
        grad_queries = product((k_ref[:, lanes] * scale).T, grad_scores).T
        p_ref[:, lanes] = grad_queries.astype(BF)
        p_ref[:, width + head * HD : width + (head + 1) * HD] = grad_keys.astype(BF)
        p_ref[:, 2 * width + head * HD : 2 * width + (head + 1) * HD] = grad_values.astype(BF)
        b_ref[0:1, lanes] = jnp.sum(grad_queries, axis=0, keepdims=True)
        b_ref[1:2, lanes] = jnp.sum(grad_values, axis=0, keepdims=True)


def attention_back(probability, queries, keys, values, blocks, gates):
    length, width = queries.shape
    heads = width // HD
    return pl.pallas_call(
        functools.partial(attention_back_kernel, heads, len(blocks)),
        out_shape=(
            jax.ShapeDtypeStruct((length, 3 * width), BF),
            jax.ShapeDtypeStruct((2, width), F32),
        ),
        in_specs=[FAR] + [VMEM] * (3 + len(blocks)) + [ANYWHERE] * len(gates),
        out_specs=(VMEM, VMEM),
        scratch_shapes=[
            pltpu.VMEM((heads, length, length), BF),
            pltpu.VMEM((length, width), BF),
            pltpu.SemaphoreType.DMA((heads,)),
        ],
        compiler_params=PARAMS,
        cost_estimate=pl.CostEstimate(
            flops=10_000_000_000, bytes_accessed=10_000_000, transcendentals=0
        ),
    )(probability, queries, keys, values, *blocks, *gates)


def place_bit(bit):
    return (lax.axis_index("context") // bit) % 2 == 0


def halves_out(value, bit, own_ref, other_ref):
    rows = own_ref.shape[0]
    low = place_bit(bit)
    own_ref[...] = jnp.where(low, value[:rows], value[rows:])
    other_ref[...] = jnp.where(low, value[rows:], value[:rows]).astype(BF)


def pair_grad_kernel(left, left_pair, right, right_pair, _, own_ref, other_ref):
    value = product_left(left[...], right[...]) + product_left(left_pair[...], right_pair[...])
    halves_out(value, 1, own_ref, other_ref)


def pair_grad(left, left_pair, right, right_pair, gate):
    shape = (left.shape[1] // 2, right.shape[1])
    return pl.pallas_call(
        pair_grad_kernel,
        out_shape=(jax.ShapeDtypeStruct(shape, F32), jax.ShapeDtypeStruct(shape, BF)),
        in_specs=[VMEM] * 4 + [ANYWHERE],
        out_specs=(VMEM,) * 2,
        compiler_params=PARAMS,
    )(left, left_pair, right, right_pair, gate)


def column_grad_kernel(extra, left, right, *refs):
    mine_ref, sent_ref = refs[-2:]
    rows, step = left.shape[1], mine_ref.shape[1]
    sent_ref[:rows] = product_left(left[...], right[:, step:]).astype(BF)
    mine_ref[:rows] = product_left(left[...], right[:, :step])
    if extra:
        low = refs[0][...].astype(BF)
        sent_ref[rows:] = low
        mine_ref[rows:] = low.astype(F32)


def column_grad(left, right, gate, extra=None):
    rows = left.shape[1] + (0 if extra is None else extra.shape[0])
    shape = (rows, right.shape[1] // 2)
    more = [] if extra is None else [extra]
    return pl.pallas_call(
        functools.partial(column_grad_kernel, len(more)),
        out_shape=(jax.ShapeDtypeStruct(shape, F32), jax.ShapeDtypeStruct(shape, BF)),
        in_specs=[VMEM] * (2 + len(more)) + [ANYWHERE],
        out_specs=(VMEM,) * 2,
        compiler_params=PARAMS,
    )(left, right, *more, gate)


def sent_grad_kernel(left, right, sums, sent_ref):
    step = left.shape[1] // 2
    sent_ref[:step] = product_left(left[:, step:], right[...]).astype(BF)
    sent_ref[step:] = jnp.zeros_like(sent_ref[step:])
    sent_ref[step : step + 2, : sums.shape[1]] = sums[...].astype(BF)


def sent_grad(left, right, sums):
    return pl.pallas_call(
        sent_grad_kernel,
        out_shape=jax.ShapeDtypeStruct((left.shape[1] // 2 + 16, right.shape[1]), BF),
        in_specs=[VMEM] * 3,
        out_specs=VMEM,
        compiler_params=PARAMS,
    )(left, right, sums)


def split_kernel(count, bit, *refs):
    value = refs[0][...].astype(F32)
    for other in refs[1:count]:
        value = value + other[...].astype(F32)
    halves_out(value, bit, *refs[-2:])


def split(values, bit, gates=()):
    shape = (values[0].shape[0] // 2, values[0].shape[1])
    return pl.pallas_call(
        functools.partial(split_kernel, len(values), bit),
        out_shape=(jax.ShapeDtypeStruct(shape, F32), jax.ShapeDtypeStruct(shape, BF)),
        in_specs=[VMEM] * len(values) + [ANYWHERE] * len(gates),
        out_specs=(VMEM,) * 2,
        compiler_params=PARAMS,
    )(*values, *gates)


def add_kernel(own_ref, other_ref, *refs):
    refs[-1][...] = (own_ref[...] + other_ref[...].astype(F32)).astype(BF)


def add_low(own, other, gates=()):
    return pl.pallas_call(
        add_kernel,
        out_shape=jax.ShapeDtypeStruct(own.shape, BF),
        in_specs=[VMEM] * 2 + [ANYWHERE] * len(gates),
        out_specs=VMEM,
        compiler_params=PARAMS,
    )(own, other, *gates)


def join_kernel(bit, own_ref, other_ref, *refs):
    rows = own_ref.shape[0]
    low = place_bit(bit)
    own, other = own_ref[...], other_ref[...]
    refs[-1][:rows] = jnp.where(low, own, other).astype(refs[-1].dtype)
    refs[-1][rows:] = jnp.where(low, other, own).astype(refs[-1].dtype)


def join(own, other, bit, dtype, gates=()):
    return pl.pallas_call(
        functools.partial(join_kernel, bit),
        out_shape=jax.ShapeDtypeStruct((2 * own.shape[0], own.shape[1]), dtype),
        in_specs=[VMEM] * 2 + [ANYWHERE] * len(gates),
        out_specs=VMEM,
        compiler_params=PARAMS,
    )(own, other, *gates)


def sums_kernel(one, two, first, normed_one, top, normed_two, _, out_ref):
    def put(row, value):
        out_ref[row : row + 1] = jnp.sum(value, axis=0, keepdims=True)

    put(0, one[...])
    put(1, two[...])
    put(2, first[...] * normed_one[...])
    put(3, top[...] * normed_two[...])
    put(4, first[...])
    put(5, top[...])


def row_sums(*operands):
    return pl.pallas_call(
        sums_kernel,
        out_shape=jax.ShapeDtypeStruct((6, operands[0].shape[1]), F32),
        in_specs=[VMEM] * 6 + [ANYWHERE],
        out_specs=VMEM,
        compiler_params=PARAMS,
    )(*operands)


def build(mesh):
    count = dict(mesh.shape)
    paired = count["weight"] == 2

    def flip(value, axis, bit):
        return lax.ppermute(value, axis, [(i, i ^ bit) for i in range(count[axis])])

    def bits(axis):
        bit, found = 1, []
        while bit < count[axis]:
            found.append(bit)
            bit *= 2
        return found

    def shards(
        tokens,
        segments,
        query_key_value_weight,
        input_bias,
        output_weight,
        row_bias,
        norm_gain,
        norm_bias,
        up_weight,
        up_bias,
        down_weight,
        cotangent,
    ):
        weight_at = lax.axis_index("weight")
        context_at = lax.axis_index("context")
        core_at = lax.axis_index("tensor") % 2
        rows, width = tokens.shape
        half = rows // 2
        shard_width = input_bias.shape[2]
        heads = shard_width // HD
        packs = count["context"]

        def columns(value):
            if not paired:
                return value
            middle = value.shape[-1] // 2
            swapped = jnp.concatenate([value[..., middle:], value[..., :middle]], axis=-1)
            return jnp.where(weight_at == 0, value, swapped)

        def own_rows(value):
            middle = value.shape[0] // 2
            swapped = jnp.concatenate([value[middle:], value[:middle]], axis=0)
            return jnp.where(core_at == 0, value, swapped)

        def swapped(value):
            return flip(value, "weight", 1)

        def gather_weight(value, axis):
            if paired:
                return [value, flip(value, "weight", 1)]
            return [lax.all_gather(value, "weight", axis=axis, tiled=True)]

        def contract(value, groups):
            step = width // len(groups)
            total = product(value[:, :step], groups[0])
            for number in range(1, len(groups)):
                total = total + product(
                    value[:, number * step : (number + 1) * step], groups[number]
                )
            return total

        def expand(value, groups):
            parts = [product(value, group) for group in groups]
            return parts[0] if len(parts) == 1 else jnp.concatenate(parts, axis=1)

        def contract_right(value, groups):
            step = width // len(groups)
            total = product_right(value[:, :step], groups[0])
            for number in range(1, len(groups)):
                total = total + product_right(
                    value[:, number * step : (number + 1) * step], groups[number]
                )
            return total

        def expand_right(value, groups):
            parts = [product_right(value, group) for group in groups]
            return parts[0] if len(parts) == 1 else jnp.concatenate(parts, axis=1)

        def row_total(partial):
            mine, theirs = partial[:half], partial[half:].astype(BF)
            total = mine + flip(theirs, "tensor", 1).astype(F32)
            for bit in bits("tensor")[1:]:
                low = total.astype(BF)
                total = low.astype(F32) + flip(low, "tensor", bit).astype(F32)
            return total, low

        def both_halves(value):
            return jnp.concatenate([value, flip(value, "tensor", 1)], axis=0)

        def take_half(value, which):
            middle = value.shape[0] // 2
            return lax.dynamic_slice_in_dim(value, which * middle, middle, axis=0)

        def context_total(value):
            return lax.psum(value.astype(BF), "context").astype(F32)

        def finish_total(halves, gates, done=0):
            order = bits("context")
            for number, bit in enumerate(order):
                if number < done:
                    continue
                received = flip(halves[1], "context", bit)
                if number + 1 < len(order):
                    halves = split([halves[0], received], order[number + 1], gates[number])
            summed = low = add_low(halves[0], received, gates[len(order) - 1])
            for number, bit in enumerate(reversed(order)):
                kind = F32 if number + 1 == len(order) else BF
                received = flip(low, "context", bit)
                low = join(low, received, bit, kind, gates[len(order) + number])
            return low, summed

        def context_blocks(value):
            blocks = [value]
            for bit in reversed(bits("context")):
                blocks = blocks + [flip(block, "context", bit) for block in blocks]
            order = [0]
            for bit in reversed(bits("context")):
                order = order + [at ^ bit for at in order]
            return [blocks[order.index(j)] for j in range(packs)]

        def in_order(blocks):
            placed = []
            for at in range(packs):
                chosen = blocks[0]
                for j in range(1, packs):
                    chosen = jnp.where(context_at == (at ^ j), blocks[j], chosen)
                placed.append(chosen)
            return jnp.concatenate(placed, axis=0)

        gains, shifts, row_pair = columns(norm_gain[0]), columns(norm_bias[0]), columns(row_bias[0])
        cotangent_rows = columns(take_half(cotangent, core_at)).astype(F32)

        projection = query_key_value_weight[0].reshape(-1, 3 * shard_width)
        input_groups = gather_weight(projection, 0)

        def with_segments(which):
            numbers = take_half(segments, which).astype(BF)
            numbers = jnp.pad(numbers[None], ((0, 15), (0, width - half)))
            return jnp.concatenate([take_half(tokens, which), numbers], axis=0)

        halves = context_blocks(with_segments(core_at))
        up_groups = gather_weight(after(up_weight[0], halves[1]), 0)
        output_groups = gather_weight(after(output_weight[0], halves[2 % packs]), 1)
        down_groups = gather_weight(after(down_weight[0], halves[3 % packs]), 1)
        others = [with_segments(1 - core_at)] + [flip(block, "tensor", 1) for block in halves[1:]]
        blocks = [block for pair in zip(halves, others) for block in pair]
        pack_queries, pack_keys, pack_values, context, pack_rows, pack_segments = front(
            blocks, input_bias[0], input_groups
        )

        def own_block(value):
            return lax.dynamic_slice_in_dim(value, context_at * rows, rows, 0)

        hidden_half = columns(take_half(tokens, core_at)).astype(F32)
        total, sent = row_total(expand(context, output_groups))
        pack_probability = probabilities(
            pack_queries, pack_keys, pack_segments, (sent, up_groups[-1])
        )
        attended = after(total, pack_probability, down_groups[-1]) + row_pair[0]
        normed_one, inverse_one = normalize(hidden_half + attended)
        first_norm = normed_one * gains[0] + shifts[0]
        first_low = both_halves(first_norm.astype(BF))

        preactivation = contract(first_low, up_groups) + up_bias[0]
        cumulative = 0.5 * (1.0 + lax.erf(preactivation * ROOT_HALF))
        activated = (preactivation * cumulative).astype(BF)
        slope = cumulative + preactivation * DENSITY_FACTOR * jnp.exp(
            -0.5 * preactivation * preactivation
        )
        total, _ = row_total(expand(activated, down_groups))
        step = width // 2
        if paired:
            first_pair = swapped(first_low[:, step:])
            total = after(total, first_pair)
        normed_two, inverse_two = normalize(first_norm + (total + row_pair[1]))
        result = (normed_two * gains[1] + shifts[1]).astype(BF)

        layer_output = columns(own_rows(both_halves(result)))
        grad_two = normalize_back(cotangent_rows, normed_two, inverse_two, gains[1])
        grad_two_low = both_halves(grad_two.astype(BF))

        def shares(left, right, axis):
            step = width // 2
            if axis == 0:
                return (
                    product_left(left[:, :step], right),
                    product_left(left[:, step:], right).astype(BF),
                )
            return (
                product_left(left, right[:, :step]),
                product_left(left, right[:, step:]).astype(BF),
            )

        def scattered(left, right, axis):
            return lax.psum_scatter(
                product_left(left, right).astype(BF), "weight", scatter_dimension=axis, tiled=True
            ).astype(F32)

        grad_pre = contract_right(grad_two_low, down_groups) * slope
        grad_pre_low = grad_pre.astype(BF)
        total, sent = row_total(expand_right(grad_pre_low, up_groups))
        if paired:
            pre_pair = swapped(grad_pre_low)
            down_mine, down_sent = column_grad(activated, grad_two_low, sent)
            down_received = swapped(down_sent)
            total = after(total, down_sent, pre_pair)
        grad_first = grad_two + total
        grad_one = normalize_back(grad_first, normed_one, inverse_one, gains[0])
        grad_one_low = both_halves(grad_one.astype(BF))
        grad_context = contract_right(grad_one_low, output_groups).astype(BF)
        grad_context_blocks = context_blocks(grad_context)

        gates = []
        if paired:
            up_halves = pair_grad(
                first_low[:, :step], first_pair, grad_pre_low, pre_pair, grad_context
            )
            up_halves = split(
                [up_halves[0], flip(up_halves[1], "context", 1)], 2, (grad_context_blocks[-1],)
            )
            down_halves = split([down_mine, down_received], 1, (grad_context_blocks[-1],))
            gates = [down_halves[1], up_halves[1], layer_output]

        pack_projected, bias_grads = attention_back(
            pack_probability, pack_queries, pack_keys, pack_values, grad_context_blocks, gates
        )
        total, final_sent = row_total(expand_right(own_block(pack_projected), input_groups))
        if paired:
            input_sent = sent_grad(pack_rows, pack_projected, bias_grads)
            received = swapped(input_sent)
            grad_input = product_left(pack_rows[:, :step], pack_projected) + received[
                :step
            ].astype(F32)
            bias_grads = bias_grads.astype(BF).astype(F32) + received[
                step : step + 2, :shard_width
            ].astype(F32)
            grad_up, up_low = finish_total(
                up_halves, [(), (pack_projected,), (), ()], 1
            )
            grad_down, down_low = finish_total(down_halves, [(pack_projected,), (), (), ()])
        else:
            grad_input = scattered(pack_rows, pack_projected, 0)
            bias_grads = lax.psum(bias_grads, "weight")
            grad_down = context_total(scattered(activated, grad_two_low, 1))
            grad_up = context_total(scattered(first_low, grad_pre_low, 0))

        small = row_sums(
            grad_one, grad_two, grad_first, normed_one, cotangent_rows, normed_two, grad_context
        )
        small = small + flip(small, "tensor", 1)
        share_width = output_weight.shape[2]
        joined = jnp.concatenate([columns(small).reshape(-1), jnp.sum(grad_pre, axis=0)])
        size = joined.shape[0]
        joined = jnp.pad(joined, (0, -size % (16 * share_width))).reshape(-1, share_width)
        out_rows, joined_rows = context.shape[1], joined.shape[0]
        if paired:
            below = -out_rows % (16 * packs * 4)
            joined = jnp.pad(joined, ((0, (below - joined_rows) % (16 * packs)), (0, 0)))
            out_mine, out_sent = column_grad(context, grad_one_low, grad_context, joined)
            out_halves = split([out_mine, swapped(out_sent)], 1, (down_low,))
            merged, _ = finish_total(out_halves, [(), (), (), ()])
        else:
            merged = jnp.concatenate(
                [
                    context_total(scattered(context, grad_one_low, 1)),
                    context_total(lax.psum(joined, "weight")),
                ],
                axis=0,
            )
        grad_out = merged[:out_rows]
        joined = merged[out_rows : out_rows + joined_rows].reshape(-1)
        small = joined[: 6 * width].reshape(3, 2, width)
        hidden_sum = joined[6 * width : size]
        grad_tokens = columns(own_rows(both_halves(grad_one + total)))
        return (
            layer_output,
            grad_tokens,
            grad_input.reshape(1, -1, 3, shard_width),
            bias_grads[None],
            grad_out[None],
            small[0][None],
            small[1][None],
            small[2][None],
            grad_up[None],
            hidden_sum[None],
            grad_down[None],
        )

    return shards


def solution(mesh):
    token_rows = P(("weight", "context"), None)
    input_spec = P(None, "weight", None, "tensor")
    out_spec = P(None, "tensor", "weight")
    placed = (
        token_rows,
        P(("weight", "context")),
        input_spec,
        P(None, None, "tensor"),
        out_spec,
        P(),
        P(),
        P(),
        P(None, "weight", "tensor"),
        P(None, "tensor"),
        out_spec,
        token_rows,
    )
    return jax.shard_map(
        build(mesh),
        mesh=mesh,
        in_specs=placed,
        out_specs=(
            token_rows,
            token_rows,
            input_spec,
            P(None, None, "tensor"),
            out_spec,
            P(),
            P(),
            P(),
            P(None, "weight", "tensor"),
            P(None, "tensor"),
            out_spec,
        ),
        check_vma=False,
    )
```

```python
import functools

import jax
import jax.experimental.pallas as pl
import jax.experimental.pallas.tpu as pltpu
import jax.numpy as jnp
from jax import lax
from jax.sharding import PartitionSpec as P

HD = 64
EPSILON = 1e-05
NEG_FILL = -1e30
ROOT_HALF = 0.7071067811865476
DENSITY_FACTOR = 0.3989422804014327
BF = jnp.bfloat16
F32 = jnp.float32


def product(left, right):
    return jnp.dot(left, right, preferred_element_type=F32)


def product_left(left, right):
    return lax.dot_general(left, right, (((0,), (0,)), ((), ())), preferred_element_type=F32)


def product_right(left, right):
    return lax.dot_general(left, right, (((1,), (1,)), ((), ())), preferred_element_type=F32)


def normalize(summed):
    center = summed - jnp.mean(summed, axis=-1, keepdims=True)
    inverse = lax.rsqrt(jnp.mean(center * center, axis=-1, keepdims=True) + EPSILON)
    return center * inverse, inverse


def normalize_back(grad_output, normed, inverse, gain_vector):
    scaled = grad_output * gain_vector
    return inverse * (
        scaled
        - jnp.mean(scaled, axis=-1, keepdims=True)
        - normed * jnp.mean(scaled * normed, axis=-1, keepdims=True)
    )


VMEM = pl.BlockSpec(memory_space=pltpu.VMEM)
FAR = pl.BlockSpec(memory_space=pltpu.HBM)
ANYWHERE = pl.BlockSpec(memory_space=pl.ANY)
PARAMS = pltpu.CompilerParams(vmem_limit_bytes=40 * 1024 * 1024)


def after(value, *others):
    zero = jnp.zeros((), F32)
    for other in others:
        first = lax.slice(other, (0,) * other.ndim, (1,) * other.ndim).reshape(())
        zero = zero + jnp.minimum(jnp.abs(first.astype(F32)), 0.0)
    return value + zero.astype(value.dtype)


def softmax_block(keys, queries, same):
    scores = jnp.where(same, product_right(keys, queries) * HD**-0.5, NEG_FILL)
    exponent = jnp.exp(scores - jnp.max(scores, axis=0, keepdims=True))
    total = jnp.sum(exponent, axis=0, keepdims=True)
    return (exponent * (1.0 / total)).astype(BF)


def as_column(row):
    return jnp.broadcast_to(row, (8, row.shape[1])).T[:, :1]


def block_start(number, rows):
    return pl.multiple_of((lax.axis_index("context") ^ number) * rows, rows)


def front_kernel(heads, packs, paired, *refs):
    blocks, refs = refs[: 2 * packs], refs[2 * packs :]
    groups = 2 if paired else 1
    b_ref, weights, refs = refs[0], refs[1 : 1 + groups], refs[1 + groups :]
    q_ref, k_ref, v_ref, c_ref, x_ref, row_ref = refs
    width = heads * HD
    model = x_ref.shape[1]
    rows = c_ref.shape[0]
    half = rows // 2
    step = model // groups
    for number in range(packs):
        for which in range(2):
            block = blocks[2 * number + which]
            at = pl.multiple_of(block_start(number, rows) + which * half, half)
            if paired:
                first = lax.axis_index("weight") == 0
                left, right = block[:half, :step], block[:half, step:]
                x_ref[pl.ds(at, half), :step] = jnp.where(first, left, right)
                x_ref[pl.ds(at, half), step:] = jnp.where(first, right, left)
            else:
                x_ref[pl.ds(at, half)] = block[:half]
            row_ref[:, pl.ds(at, half)] = block[half : half + 1, :half].astype(F32)
    for number, (out_ref, bias) in enumerate(((q_ref, 0), (k_ref, None), (v_ref, 1))):
        total = None
        for group in range(groups):
            part = product(
                x_ref[:, group * step : (group + 1) * step],
                weights[group][:, number * width : (number + 1) * width],
            )
            total = part if total is None else total + part
        if bias is not None:
            total = total + b_ref[bias : bias + 1]
        out_ref[...] = total.astype(BF)
    at = block_start(0, rows)
    same = as_column(row_ref[...]) == row_ref[:, pl.ds(at, rows)]
    for head in range(heads):
        lanes = slice(head * HD, (head + 1) * HD)
        probability = softmax_block(k_ref[:, lanes], q_ref[pl.ds(at, rows), lanes], same)
        c_ref[:, lanes] = product(v_ref[:, lanes].T, probability).T.astype(BF)


def front(blocks, biases, groups):
    packs = len(blocks) // 2
    rows = 2 * (blocks[0].shape[0] - 16)
    model = blocks[0].shape[1]
    width = biases.shape[1]
    whole = jax.ShapeDtypeStruct((packs * rows, width), BF)
    return pl.pallas_call(
        functools.partial(front_kernel, width // HD, packs, len(groups) == 2),
        out_shape=(
            whole,
            whole,
            whole,
            jax.ShapeDtypeStruct((rows, width), BF),
            jax.ShapeDtypeStruct((packs * rows, model), BF),
            jax.ShapeDtypeStruct((1, packs * rows), F32),
        ),
        in_specs=[VMEM] * (2 * packs + 1 + len(groups)),
        out_specs=(VMEM,) * 6,
        compiler_params=PARAMS,
    )(*blocks, biases, *groups)


def probability_kernel(heads, block, q_ref, k_ref, row_ref, *refs):
    a_hbm, token_ref, a_ref, copy_sems = refs[-4:]
    token_ref[...] = jnp.minimum(jnp.abs(row_ref[:, : token_ref.shape[1]]), 0.0)
    count = q_ref.shape[0] // block

    def copy(number):
        at = pl.multiple_of(number * block, block)
        return pltpu.make_async_copy(
            a_ref.at[:, :, pl.ds(at, block)],
            a_hbm.at[:, :, pl.ds(at, block)],
            copy_sems.at[number],
        )

    def body(number, carry):
        at = pl.multiple_of(number * block, block)
        same = as_column(row_ref[...]) == row_ref[:, pl.ds(at, block)]
        for head in range(heads):
            lanes = slice(head * HD, (head + 1) * HD)
            a_ref[head, :, pl.ds(at, block)] = softmax_block(
                k_ref[:, lanes], q_ref[pl.ds(at, block), lanes], same
            )
        copy(number).start()
        return carry

    lax.fori_loop(0, count, body, 0)
    for number in range(count):
        copy(number).wait()


def probabilities(queries, keys, segments, gates):
    length, width = queries.shape
    heads = width // HD
    block = 256
    return pl.pallas_call(
        functools.partial(probability_kernel, heads, block),
        out_shape=(
            pltpu.HBM((heads, length, length), BF),
            jax.ShapeDtypeStruct((1, 128), F32),
        ),
        in_specs=[VMEM] * 3 + [ANYWHERE] * len(gates),
        out_specs=(FAR, VMEM),
        scratch_shapes=[
            pltpu.VMEM((heads, length, length), BF),
            pltpu.SemaphoreType.DMA((length // block,)),
        ],
        compiler_params=PARAMS,
    )(queries, keys, segments, *gates)


def attention_back_kernel(heads, packs, a_hbm, q_ref, k_ref, v_ref, *refs):
    blocks, (p_ref, b_ref, a_ref, c_ref, copy_sems) = refs[:packs], refs[-5:]
    width = heads * HD
    scale = jnp.asarray(HD**-0.5, BF)
    copies = [
        pltpu.make_async_copy(a_hbm.at[head], a_ref.at[head], copy_sems.at[head])
        for head in range(heads)
    ]
    for copy in copies:
        copy.start()
    for number, block in enumerate(blocks):
        rows = block.shape[0]
        c_ref[pl.ds(block_start(number, rows), rows)] = block[...]
    for head in range(heads):
        lanes = slice(head * HD, (head + 1) * HD)
        grad_context = c_ref[:, lanes]
        copies[head].wait()
        low = a_ref[head]
        wide = low.astype(F32)
        weighted = wide * product_right(v_ref[:, lanes], grad_context)
        row_dot = jnp.sum(weighted, axis=0, keepdims=True)
        grad_scores = (weighted - wide * row_dot).astype(BF)
        grad_values = product(low, grad_context)
        grad_keys = product(grad_scores, q_ref[:, lanes] * scale)
        grad_queries = product((k_ref[:, lanes] * scale).T, grad_scores).T
        p_ref[:, lanes] = grad_queries.astype(BF)
        p_ref[:, width + head * HD : width + (head + 1) * HD] = grad_keys.astype(BF)
        p_ref[:, 2 * width + head * HD : 2 * width + (head + 1) * HD] = grad_values.astype(BF)
        b_ref[0:1, lanes] = jnp.sum(grad_queries, axis=0, keepdims=True)
        b_ref[1:2, lanes] = jnp.sum(grad_values, axis=0, keepdims=True)


def attention_back(probability, queries, keys, values, blocks, gates):
    length, width = queries.shape
    heads = width // HD
    return pl.pallas_call(
        functools.partial(attention_back_kernel, heads, len(blocks)),
        out_shape=(
            jax.ShapeDtypeStruct((length, 3 * width), BF),
            jax.ShapeDtypeStruct((2, width), F32),
        ),
        in_specs=[FAR] + [VMEM] * (3 + len(blocks)) + [ANYWHERE] * len(gates),
        out_specs=(VMEM, VMEM),
        scratch_shapes=[
            pltpu.VMEM((heads, length, length), BF),
            pltpu.VMEM((length, width), BF),
            pltpu.SemaphoreType.DMA((heads,)),
        ],
        compiler_params=PARAMS,
        cost_estimate=pl.CostEstimate(
            flops=10_000_000_000, bytes_accessed=10_000_000, transcendentals=0
        ),
    )(probability, queries, keys, values, *blocks, *gates)


def place_bit(bit):
    return (lax.axis_index("context") // bit) % 2 == 0


def halves_out(value, bit, own_ref, other_ref):
    rows = own_ref.shape[0]
    low = place_bit(bit)
    own_ref[...] = jnp.where(low, value[:rows], value[rows:])
    other_ref[...] = jnp.where(low, value[rows:], value[:rows]).astype(BF)


def pair_grad_kernel(left, left_pair, right, right_pair, _, own_ref, other_ref):
    value = product_left(left[...], right[...]) + product_left(left_pair[...], right_pair[...])
    halves_out(value, 1, own_ref, other_ref)


def pair_grad(left, left_pair, right, right_pair, gate):
    shape = (left.shape[1] // 2, right.shape[1])
    return pl.pallas_call(
        pair_grad_kernel,
        out_shape=(jax.ShapeDtypeStruct(shape, F32), jax.ShapeDtypeStruct(shape, BF)),
        in_specs=[VMEM] * 4 + [ANYWHERE],
        out_specs=(VMEM,) * 2,
        compiler_params=PARAMS,
    )(left, left_pair, right, right_pair, gate)


def column_grad_kernel(extra, left, right, *refs):
    mine_ref, sent_ref = refs[-2:]
    rows, step = left.shape[1], mine_ref.shape[1]
    sent_ref[:rows] = product_left(left[...], right[:, step:]).astype(BF)
    mine_ref[:rows] = product_left(left[...], right[:, :step])
    if extra:
        low = refs[0][...].astype(BF)
        sent_ref[rows:] = low
        mine_ref[rows:] = low.astype(F32)


def column_grad(left, right, gate, extra=None):
    rows = left.shape[1] + (0 if extra is None else extra.shape[0])
    shape = (rows, right.shape[1] // 2)
    more = [] if extra is None else [extra]
    return pl.pallas_call(
        functools.partial(column_grad_kernel, len(more)),
        out_shape=(jax.ShapeDtypeStruct(shape, F32), jax.ShapeDtypeStruct(shape, BF)),
        in_specs=[VMEM] * (2 + len(more)) + [ANYWHERE],
        out_specs=(VMEM,) * 2,
        compiler_params=PARAMS,
    )(left, right, *more, gate)


def sent_grad_kernel(left, right, sums, *refs):
    sent_ref = refs[-1]
    step = left.shape[1] // 2
    sent_ref[:step] = product_left(left[:, step:], right[...]).astype(BF)
    sent_ref[step:] = jnp.zeros_like(sent_ref[step:])
    sent_ref[step : step + 2, : sums.shape[1]] = sums[...].astype(BF)


def sent_grad(left, right, sums, gates):
    return pl.pallas_call(
        sent_grad_kernel,
        out_shape=jax.ShapeDtypeStruct((left.shape[1] // 2 + 16, right.shape[1]), BF),
        in_specs=[VMEM] * 3 + [ANYWHERE] * len(gates),
        out_specs=VMEM,
        compiler_params=PARAMS,
    )(left, right, sums, *gates)


def split_kernel(count, bit, *refs):
    value = refs[0][...].astype(F32)
    for other in refs[1:count]:
        value = value + other[...].astype(F32)
    halves_out(value, bit, *refs[-2:])


def split(values, bit, gates=()):
    shape = (values[0].shape[0] // 2, values[0].shape[1])
    return pl.pallas_call(
        functools.partial(split_kernel, len(values), bit),
        out_shape=(jax.ShapeDtypeStruct(shape, F32), jax.ShapeDtypeStruct(shape, BF)),
        in_specs=[VMEM] * len(values) + [ANYWHERE] * len(gates),
        out_specs=(VMEM,) * 2,
        compiler_params=PARAMS,
    )(*values, *gates)


def split_parts_kernel(parts, merged, bit, *refs):
    own_ref, other_ref = refs[-2:]
    low = place_bit(bit)
    start = 0
    for number, rows in enumerate(parts):
        if merged:
            value = refs[0][start : start + rows] + refs[1][start : start + rows].astype(F32)
        else:
            value = refs[2 * number][...] + refs[2 * number + 1][...].astype(F32)
        first, second = value[: rows // 2], value[rows // 2 :]
        at = slice(start // 2, (start + rows) // 2)
        own_ref[at] = jnp.where(low, first, second)
        other_ref[at] = jnp.where(low, second, first).astype(BF)
        start += rows


def split_parts(values, parts, bit, gates):
    merged = len(values) == 2
    shape = (sum(parts) // 2, values[0].shape[1])
    return pl.pallas_call(
        functools.partial(split_parts_kernel, parts, merged, bit),
        out_shape=(jax.ShapeDtypeStruct(shape, F32), jax.ShapeDtypeStruct(shape, BF)),
        in_specs=[VMEM] * len(values) + [ANYWHERE] * len(gates),
        out_specs=(VMEM,) * 2,
        compiler_params=PARAMS,
    )(*values, *gates)


def join_parts_kernel(parts, last, bit, own_ref, other_ref, *refs):
    low = place_bit(bit)
    start = 0
    for number, rows in enumerate(parts):
        at = slice(start, start + rows)
        own, other = own_ref[at], other_ref[at]
        ref, base = (refs[number], 0) if last else (refs[0], 2 * start)
        ref[base : base + rows] = jnp.where(low, own, other).astype(ref.dtype)
        ref[base + rows : base + 2 * rows] = jnp.where(low, other, own).astype(ref.dtype)
        start += rows


def join_parts(own, other, parts, bit, last):
    columns = own.shape[1]
    if last:
        shapes = tuple(jax.ShapeDtypeStruct((2 * rows, columns), F32) for rows in parts)
    else:
        shapes = (jax.ShapeDtypeStruct((2 * own.shape[0], columns), BF),)
    return pl.pallas_call(
        functools.partial(join_parts_kernel, parts, last, bit),
        out_shape=shapes,
        in_specs=[VMEM] * 2,
        out_specs=(VMEM,) * len(shapes),
        compiler_params=PARAMS,
    )(own, other)


def finish_kernel(parts, own_ref, other_ref, down_ref, out_ref, *small_refs):
    low = place_bit(1)
    joined = []
    start = 0
    for rows in parts:
        own, other = own_ref[start : start + rows], other_ref[start : start + rows]
        joined.append((jnp.where(low, own, other), jnp.where(low, other, own)))
        start += rows
    for number in range(2):
        down_ref[number * parts[0] : (number + 1) * parts[0]] = joined[0][number].astype(F32)
    value = jnp.concatenate([part.astype(F32) for part in joined[1]], axis=0)
    at = out_ref.shape[0]
    out_ref[...] = value[:at]
    step = value.shape[1]
    for ref in small_refs:
        for row in range(ref.shape[0]):
            for piece in range(ref.shape[1] // step):
                ref[row : row + 1, piece * step : (piece + 1) * step] = value[at : at + 1]
                at += 1


def finish(own, other, parts, out_rows, width, hidden):
    columns = own.shape[1]
    shapes = [(2 * parts[0], columns), (out_rows, columns)] + [(2, width)] * 3 + [(1, hidden)]
    return pl.pallas_call(
        functools.partial(finish_kernel, parts),
        out_shape=tuple(jax.ShapeDtypeStruct(shape, F32) for shape in shapes),
        in_specs=[VMEM] * 2,
        out_specs=(VMEM,) * len(shapes),
        compiler_params=PARAMS,
    )(own, other)


def add_wide_kernel(first_ref, second_ref, *refs):
    refs[-1][...] = first_ref[...].astype(F32) + second_ref[...].astype(F32)


def add_wide(first, second, gates):
    return pl.pallas_call(
        add_wide_kernel,
        out_shape=jax.ShapeDtypeStruct(first.shape, F32),
        in_specs=[VMEM] * 2 + [ANYWHERE] * len(gates),
        out_specs=VMEM,
        compiler_params=PARAMS,
    )(first, second, *gates)


def add_kernel(own_ref, other_ref, *refs):
    refs[-1][...] = (own_ref[...] + other_ref[...].astype(F32)).astype(BF)


def add_low(own, other, gates=()):
    return pl.pallas_call(
        add_kernel,
        out_shape=jax.ShapeDtypeStruct(own.shape, BF),
        in_specs=[VMEM] * 2 + [ANYWHERE] * len(gates),
        out_specs=VMEM,
        compiler_params=PARAMS,
    )(own, other, *gates)


def join_kernel(bit, own_ref, other_ref, *refs):
    rows = own_ref.shape[0]
    low = place_bit(bit)
    own, other = own_ref[...], other_ref[...]
    refs[-1][:rows] = jnp.where(low, own, other).astype(refs[-1].dtype)
    refs[-1][rows:] = jnp.where(low, other, own).astype(refs[-1].dtype)


def join(own, other, bit, dtype, gates=()):
    return pl.pallas_call(
        functools.partial(join_kernel, bit),
        out_shape=jax.ShapeDtypeStruct((2 * own.shape[0], own.shape[1]), dtype),
        in_specs=[VMEM] * 2 + [ANYWHERE] * len(gates),
        out_specs=VMEM,
        compiler_params=PARAMS,
    )(own, other, *gates)


def sums_kernel(one, two, first, normed_one, top, normed_two, _, out_ref):
    def put(row, value):
        out_ref[row : row + 1] = jnp.sum(value, axis=0, keepdims=True)

    put(0, one[...])
    put(1, two[...])
    put(2, first[...] * normed_one[...])
    put(3, top[...] * normed_two[...])
    put(4, first[...])
    put(5, top[...])


def row_sums(*operands):
    return pl.pallas_call(
        sums_kernel,
        out_shape=jax.ShapeDtypeStruct((6, operands[0].shape[1]), F32),
        in_specs=[VMEM] * 6 + [ANYWHERE],
        out_specs=VMEM,
        compiler_params=PARAMS,
    )(*operands)


def build(mesh):
    count = dict(mesh.shape)
    paired = count["weight"] == 2

    def flip(value, axis, bit):
        return lax.ppermute(value, axis, [(i, i ^ bit) for i in range(count[axis])])

    def bits(axis):
        bit, found = 1, []
        while bit < count[axis]:
            found.append(bit)
            bit *= 2
        return found

    def shards(
        tokens,
        segments,
        query_key_value_weight,
        input_bias,
        output_weight,
        row_bias,
        norm_gain,
        norm_bias,
        up_weight,
        up_bias,
        down_weight,
        cotangent,
    ):
        weight_at = lax.axis_index("weight")
        context_at = lax.axis_index("context")
        core_at = lax.axis_index("tensor") % 2
        rows, width = tokens.shape
        half = rows // 2
        shard_width = input_bias.shape[2]
        heads = shard_width // HD
        packs = count["context"]

        def columns(value):
            if not paired:
                return value
            middle = value.shape[-1] // 2
            swapped = jnp.concatenate([value[..., middle:], value[..., :middle]], axis=-1)
            return jnp.where(weight_at == 0, value, swapped)

        def own_rows(value):
            middle = value.shape[0] // 2
            swapped = jnp.concatenate([value[middle:], value[:middle]], axis=0)
            return jnp.where(core_at == 0, value, swapped)

        def swapped(value):
            return flip(value, "weight", 1)

        def gather_weight(value, axis):
            if paired:
                return [value, flip(value, "weight", 1)]
            return [lax.all_gather(value, "weight", axis=axis, tiled=True)]

        def contract(value, groups):
            step = width // len(groups)
            total = product(value[:, :step], groups[0])
            for number in range(1, len(groups)):
                total = total + product(
                    value[:, number * step : (number + 1) * step], groups[number]
                )
            return total

        def expand(value, groups):
            parts = [product(value, group) for group in groups]
            return parts[0] if len(parts) == 1 else jnp.concatenate(parts, axis=1)

        def contract_right(value, groups):
            step = width // len(groups)
            total = product_right(value[:, :step], groups[0])
            for number in range(1, len(groups)):
                total = total + product_right(
                    value[:, number * step : (number + 1) * step], groups[number]
                )
            return total

        def expand_right(value, groups):
            parts = [product_right(value, group) for group in groups]
            return parts[0] if len(parts) == 1 else jnp.concatenate(parts, axis=1)

        def row_total(partial, gates=()):
            mine, theirs = partial[:half], partial[half:].astype(BF)
            received = flip(theirs, "tensor", 1)
            total = add_wide(mine, received, gates) if gates else mine + received.astype(F32)
            for bit in bits("tensor")[1:-1]:
                low = total.astype(BF)
                total = low.astype(F32) + flip(low, "tensor", bit).astype(F32)
            low = total.astype(BF)
            return low, flip(low, "tensor", bits("tensor")[-1])

        def both_halves(value):
            return jnp.concatenate([value, flip(value, "tensor", 1)], axis=0)

        def take_half(value, which):
            middle = value.shape[0] // 2
            return lax.dynamic_slice_in_dim(value, which * middle, middle, axis=0)

        def context_total(value):
            return lax.psum(value.astype(BF), "context").astype(F32)

        def context_blocks(value):
            blocks = [value]
            for bit in reversed(bits("context")):
                blocks = blocks + [flip(block, "context", bit) for block in blocks]
            order = [0]
            for bit in reversed(bits("context")):
                order = order + [at ^ bit for at in order]
            return [blocks[order.index(j)] for j in range(packs)]

        def in_order(blocks):
            placed = []
            for at in range(packs):
                chosen = blocks[0]
                for j in range(1, packs):
                    chosen = jnp.where(context_at == (at ^ j), blocks[j], chosen)
                placed.append(chosen)
            return jnp.concatenate(placed, axis=0)

        gains, shifts, row_pair = columns(norm_gain[0]), columns(norm_bias[0]), columns(row_bias[0])
        cotangent_rows = columns(take_half(cotangent, core_at)).astype(F32)

        projection = query_key_value_weight[0].reshape(-1, 3 * shard_width)
        input_groups = gather_weight(projection, 0)

        def with_segments(which):
            numbers = take_half(segments, which).astype(BF)
            numbers = jnp.pad(numbers[None], ((0, 15), (0, width - half)))
            return jnp.concatenate([take_half(tokens, which), numbers], axis=0)

        halves = context_blocks(with_segments(core_at))
        up_groups = gather_weight(after(up_weight[0], halves[2 % packs]), 0)
        output_groups = gather_weight(after(output_weight[0], halves[2 % packs]), 1)
        down_groups = gather_weight(after(down_weight[0], halves[2 % packs]), 1)
        others = [with_segments(1 - core_at)] + [flip(block, "tensor", 1) for block in halves[1:]]
        blocks = [block for pair in zip(halves, others) for block in pair]
        pack_queries, pack_keys, pack_values, context, pack_rows, pack_segments = front(
            blocks, input_bias[0], input_groups
        )

        def own_block(value):
            return lax.dynamic_slice_in_dim(value, context_at * rows, rows, 0)

        hidden_half = columns(take_half(tokens, core_at)).astype(F32)
        sent, received = row_total(expand(context, output_groups))
        pack_probability, token = probabilities(
            pack_queries, pack_keys, pack_segments, (sent, up_groups[-1])
        )
        attended = add_wide(sent, received, (token, down_groups[-1])) + row_pair[0]
        normed_one, inverse_one = normalize(hidden_half + attended)
        first_norm = normed_one * gains[0] + shifts[0]
        first_low = both_halves(first_norm.astype(BF))

        preactivation = contract(first_low, up_groups) + up_bias[0]
        cumulative = 0.5 * (1.0 + lax.erf(preactivation * ROOT_HALF))
        activated = (preactivation * cumulative).astype(BF)
        slope = cumulative + preactivation * DENSITY_FACTOR * jnp.exp(
            -0.5 * preactivation * preactivation
        )
        sent, received = row_total(expand(activated, down_groups))
        step = width // 2
        gates = ()
        if paired:
            first_pair = swapped(first_low[:, step:])
            gates = (first_pair,)
        total = add_wide(sent, received, gates)
        normed_two, inverse_two = normalize(first_norm + (total + row_pair[1]))
        result = (normed_two * gains[1] + shifts[1]).astype(BF)

        layer_output = columns(own_rows(both_halves(result)))
        grad_two = normalize_back(cotangent_rows, normed_two, inverse_two, gains[1])
        grad_two_low = both_halves(grad_two.astype(BF))

        def shares(left, right, axis):
            step = width // 2
            if axis == 0:
                return (
                    product_left(left[:, :step], right),
                    product_left(left[:, step:], right).astype(BF),
                )
            return (
                product_left(left, right[:, :step]),
                product_left(left, right[:, step:]).astype(BF),
            )

        def scattered(left, right, axis):
            return lax.psum_scatter(
                product_left(left, right).astype(BF), "weight", scatter_dimension=axis, tiled=True
            ).astype(F32)

        grad_pre = contract_right(grad_two_low, down_groups) * slope
        grad_pre_low = grad_pre.astype(BF)
        sent, received = row_total(expand_right(grad_pre_low, up_groups))
        gates = ()
        if paired:
            pre_pair = swapped(grad_pre_low)
            down_mine, down_sent = column_grad(activated, grad_two_low, sent)
            down_received = swapped(down_sent)
            gates = (down_sent, pre_pair)
            up_halves = pair_grad(first_low[:, :step], first_pair, grad_pre_low, pre_pair, sent)
        grad_first = grad_two + add_wide(sent, received, gates)
        grad_one = normalize_back(grad_first, normed_one, inverse_one, gains[0])
        grad_one_low = both_halves(grad_one.astype(BF))
        grad_context = contract_right(grad_one_low, output_groups).astype(BF)
        grad_context_blocks = context_blocks(grad_context)

        small = row_sums(
            grad_one, grad_two, grad_first, normed_one, cotangent_rows, normed_two, grad_context
        )
        small = small + flip(small, "tensor", 1)
        share_width = output_weight.shape[2]
        joined = jnp.concatenate([columns(small).reshape(-1), jnp.sum(grad_pre, axis=0)])
        size = joined.shape[0]
        joined = jnp.pad(joined, (0, -size % (16 * share_width))).reshape(-1, share_width)
        out_rows, joined_rows = context.shape[1], joined.shape[0]
        chained = paired and packs == 4
        gates = []
        if chained:
            up_halves = split(
                [up_halves[0], flip(up_halves[1], "context", 1)], 2, (grad_context_blocks[2],)
            )
            last = (grad_context_blocks[-1],)
            below = -out_rows % 256
            joined = jnp.pad(joined, ((0, below - joined_rows), (0, 0)))
            out_mine, out_sent = column_grad(context, grad_one_low, grad_context, joined)
            parts = (down_mine.shape[0], out_mine.shape[0])
            halves = split_parts(
                (down_mine, down_received, out_mine, swapped(out_sent)), parts, 1, last
            )
            gates = [halves[1], up_halves[1], layer_output]

        pack_projected, bias_grads = attention_back(
            pltpu.with_memory_space_constraint(pack_probability, pltpu.HBM),
            pack_queries,
            pack_keys,
            pack_values,
            grad_context_blocks,
            gates,
        )
        ends = ()
        if chained:
            parts = tuple(rows // 2 for rows in parts)
            halves = split_parts(
                (halves[0], flip(halves[1], "context", 1)), parts, 2, (pack_projected,)
            )
            ends = (up_halves[1], halves[1])
            input_sent = sent_grad(
                pack_rows, pack_projected, bias_grads, (up_halves[1], halves[1])
            )
            low = add_low(up_halves[0], flip(up_halves[1], "context", 2))
            low = join(low, flip(low, "context", 2), 2, BF)
            grad_up = join(low, flip(low, "context", 1), 1, F32)
            low = add_low(halves[0], flip(halves[1], "context", 2))
            small_parts = tuple(rows // 2 for rows in parts)
            (low,) = join_parts(low, flip(low, "context", 2), small_parts, 2, False)
            grad_down, grad_out, *small, hidden_sum = finish(
                low, flip(low, "context", 1), parts, out_rows, width, up_bias.shape[1]
            )
            received = swapped(input_sent)
            grad_input = product_left(pack_rows[:, :step], pack_projected) + received[
                :step
            ].astype(F32)
            bias_grads = bias_grads.astype(BF).astype(F32) + received[
                step : step + 2, :shard_width
            ].astype(F32)
        else:
            grad_input = scattered(pack_rows, pack_projected, 0)
            bias_grads = lax.psum(bias_grads, "weight")
            grad_down = context_total(scattered(activated, grad_two_low, 1))
            grad_up = context_total(scattered(first_low, grad_pre_low, 0))
            grad_out = context_total(scattered(context, grad_one_low, 1))
            joined = lax.psum(lax.psum(joined, "weight"), "context").reshape(-1)
            small = joined[: 6 * width].reshape(3, 2, width)
            hidden_sum = joined[None, 6 * width : size]
        sent, received = row_total(expand_right(own_block(pack_projected), input_groups), ends)
        total = sent.astype(F32) + received.astype(F32)
        grad_tokens = columns(own_rows(both_halves(grad_one + total)))
        return (
            layer_output,
            grad_tokens,
            grad_input.reshape(1, -1, 3, shard_width),
            bias_grads[None],
            grad_out[None],
            small[0][None],
            small[1][None],
            small[2][None],
            grad_up[None],
            hidden_sum,
            grad_down[None],
        )

    return shards


def solution(mesh):
    token_rows = P(("weight", "context"), None)
    input_spec = P(None, "weight", None, "tensor")
    out_spec = P(None, "tensor", "weight")
    placed = (
        token_rows,
        P(("weight", "context")),
        input_spec,
        P(None, None, "tensor"),
        out_spec,
        P(),
        P(),
        P(),
        P(None, "weight", "tensor"),
        P(None, "tensor"),
        out_spec,
        token_rows,
    )
    return jax.shard_map(
        build(mesh),
        mesh=mesh,
        in_specs=placed,
        out_specs=(
            token_rows,
            token_rows,
            input_spec,
            P(None, None, "tensor"),
            out_spec,
            P(),
            P(),
            P(),
            P(None, "weight", "tensor"),
            P(None, "tensor"),
            out_spec,
        ),
        check_vma=False,
    )
```

```python
import functools

import jax
import jax.experimental.pallas as pl
import jax.experimental.pallas.tpu as pltpu
import jax.numpy as jnp
from jax import lax
from jax.sharding import PartitionSpec as P

HD = 64
EPSILON = 1e-05
NEG_FILL = -1e30
ROOT_HALF = 0.7071067811865476
DENSITY_FACTOR = 0.3989422804014327
BF = jnp.bfloat16
F32 = jnp.float32


def product(left, right):
    return jnp.dot(left, right, preferred_element_type=F32)


def product_left(left, right):
    return lax.dot_general(left, right, (((0,), (0,)), ((), ())), preferred_element_type=F32)


def product_right(left, right):
    return lax.dot_general(left, right, (((1,), (1,)), ((), ())), preferred_element_type=F32)


def normalize(summed):
    center = summed - jnp.mean(summed, axis=-1, keepdims=True)
    inverse = lax.rsqrt(jnp.mean(center * center, axis=-1, keepdims=True) + EPSILON)
    return center * inverse, inverse


def normalize_back(grad_output, normed, inverse, gain_vector):
    scaled = grad_output * gain_vector
    return inverse * (
        scaled
        - jnp.mean(scaled, axis=-1, keepdims=True)
        - normed * jnp.mean(scaled * normed, axis=-1, keepdims=True)
    )


VMEM = pl.BlockSpec(memory_space=pltpu.VMEM)
FAR = pl.BlockSpec(memory_space=pltpu.HBM)
ANYWHERE = pl.BlockSpec(memory_space=pl.ANY)
PARAMS = pltpu.CompilerParams(vmem_limit_bytes=40 * 1024 * 1024)


def after(value, *others):
    zero = jnp.zeros((), F32)
    for other in others:
        first = lax.slice(other, (0,) * other.ndim, (1,) * other.ndim).reshape(())
        zero = zero + jnp.minimum(jnp.abs(first.astype(F32)), 0.0)
    return value + zero.astype(value.dtype)


def softmax_block(keys, queries, same):
    scores = jnp.where(same, product_right(keys, queries) * HD**-0.5, NEG_FILL)
    exponent = jnp.exp(scores - jnp.max(scores, axis=0, keepdims=True))
    total = jnp.sum(exponent, axis=0, keepdims=True)
    return (exponent * (1.0 / total)).astype(BF)


def as_column(row):
    return jnp.broadcast_to(row, (8, row.shape[1])).T[:, :1]


def block_start(number, rows):
    return pl.multiple_of((lax.axis_index("context") ^ number) * rows, rows)


def front_kernel(heads, packs, paired, *refs):
    blocks, refs = refs[: 2 * packs], refs[2 * packs :]
    groups = 2 if paired else 1
    b_ref, weights, refs = refs[0], refs[1 : 1 + groups], refs[1 + groups :]
    q_ref, k_ref, v_ref, c_ref, x_ref, row_ref = refs
    width = heads * HD
    model = x_ref.shape[1]
    rows = c_ref.shape[0]
    half = rows // 2
    step = model // groups
    for number in range(packs):
        for which in range(2):
            block = blocks[2 * number + which]
            at = pl.multiple_of(block_start(number, rows) + which * half, half)
            if paired:
                first = lax.axis_index("weight") == 0
                left, right = block[:half, :step], block[:half, step:]
                x_ref[pl.ds(at, half), :step] = jnp.where(first, left, right)
                x_ref[pl.ds(at, half), step:] = jnp.where(first, right, left)
            else:
                x_ref[pl.ds(at, half)] = block[:half]
            row_ref[:, pl.ds(at, half)] = block[half : half + 1, :half].astype(F32)
    for number, (out_ref, bias) in enumerate(((q_ref, 0), (k_ref, None), (v_ref, 1))):
        total = None
        for group in range(groups):
            part = product(
                x_ref[:, group * step : (group + 1) * step],
                weights[group][:, number * width : (number + 1) * width],
            )
            total = part if total is None else total + part
        if bias is not None:
            total = total + b_ref[bias : bias + 1]
        out_ref[...] = total.astype(BF)
    at = block_start(0, rows)
    same = as_column(row_ref[...]) == row_ref[:, pl.ds(at, rows)]
    for head in range(heads):
        lanes = slice(head * HD, (head + 1) * HD)
        probability = softmax_block(k_ref[:, lanes], q_ref[pl.ds(at, rows), lanes], same)
        c_ref[:, lanes] = product(v_ref[:, lanes].T, probability).T.astype(BF)


def front(blocks, biases, groups):
    packs = len(blocks) // 2
    rows = 2 * (blocks[0].shape[0] - 16)
    model = blocks[0].shape[1]
    width = biases.shape[1]
    whole = jax.ShapeDtypeStruct((packs * rows, width), BF)
    return pl.pallas_call(
        functools.partial(front_kernel, width // HD, packs, len(groups) == 2),
        out_shape=(
            whole,
            whole,
            whole,
            jax.ShapeDtypeStruct((rows, width), BF),
            jax.ShapeDtypeStruct((packs * rows, model), BF),
            jax.ShapeDtypeStruct((1, packs * rows), F32),
        ),
        in_specs=[VMEM] * (2 * packs + 1 + len(groups)),
        out_specs=(VMEM,) * 6,
        compiler_params=PARAMS,
    )(*blocks, biases, *groups)


def probability_kernel(heads, block, q_ref, k_ref, row_ref, *refs):
    a_hbm, token_ref, a_ref, copy_sems = refs[-4:]
    token_ref[...] = jnp.minimum(jnp.abs(row_ref[:, : token_ref.shape[1]]), 0.0)
    count = q_ref.shape[0] // block

    def copy(number):
        at = pl.multiple_of(number * block, block)
        return pltpu.make_async_copy(
            a_ref.at[:, :, pl.ds(at, block)],
            a_hbm.at[:, :, pl.ds(at, block)],
            copy_sems.at[number],
        )

    def body(number, carry):
        at = pl.multiple_of(number * block, block)
        same = as_column(row_ref[...]) == row_ref[:, pl.ds(at, block)]
        for head in range(heads):
            lanes = slice(head * HD, (head + 1) * HD)
            a_ref[head, :, pl.ds(at, block)] = softmax_block(
                k_ref[:, lanes], q_ref[pl.ds(at, block), lanes], same
            )
        copy(number).start()
        return carry

    lax.fori_loop(0, count, body, 0)
    for number in range(count):
        copy(number).wait()


def probabilities(queries, keys, segments, gates):
    length, width = queries.shape
    heads = width // HD
    block = 256
    return pl.pallas_call(
        functools.partial(probability_kernel, heads, block),
        out_shape=(
            pltpu.HBM((heads, length, length), BF),
            jax.ShapeDtypeStruct((1, 128), F32),
        ),
        in_specs=[VMEM] * 3 + [ANYWHERE] * len(gates),
        out_specs=(FAR, VMEM),
        scratch_shapes=[
            pltpu.VMEM((heads, length, length), BF),
            pltpu.SemaphoreType.DMA((length // block,)),
        ],
        compiler_params=PARAMS,
    )(queries, keys, segments, *gates)


def attention_back_kernel(heads, packs, a_hbm, q_ref, k_ref, v_ref, *refs):
    blocks, (p_ref, b_ref, a_ref, c_ref, copy_sems) = refs[:packs], refs[-5:]
    width = heads * HD
    scale = jnp.asarray(HD**-0.5, BF)
    copies = [
        pltpu.make_async_copy(a_hbm.at[head], a_ref.at[head], copy_sems.at[head])
        for head in range(heads)
    ]
    for copy in copies:
        copy.start()
    for number, block in enumerate(blocks):
        rows = block.shape[0]
        c_ref[pl.ds(block_start(number, rows), rows)] = block[...]
    for head in range(heads):
        lanes = slice(head * HD, (head + 1) * HD)
        grad_context = c_ref[:, lanes]
        copies[head].wait()
        low = a_ref[head]
        wide = low.astype(F32)
        weighted = wide * product_right(v_ref[:, lanes], grad_context)
        row_dot = jnp.sum(weighted, axis=0, keepdims=True)
        grad_scores = (weighted - wide * row_dot).astype(BF)
        grad_values = product(low, grad_context)
        grad_keys = product(grad_scores, q_ref[:, lanes] * scale)
        grad_queries = product((k_ref[:, lanes] * scale).T, grad_scores).T
        p_ref[:, lanes] = grad_queries.astype(BF)
        p_ref[:, width + head * HD : width + (head + 1) * HD] = grad_keys.astype(BF)
        p_ref[:, 2 * width + head * HD : 2 * width + (head + 1) * HD] = grad_values.astype(BF)
        b_ref[0:1, lanes] = jnp.sum(grad_queries, axis=0, keepdims=True)
        b_ref[1:2, lanes] = jnp.sum(grad_values, axis=0, keepdims=True)


def attention_back(probability, queries, keys, values, blocks, gates):
    length, width = queries.shape
    heads = width // HD
    return pl.pallas_call(
        functools.partial(attention_back_kernel, heads, len(blocks)),
        out_shape=(
            jax.ShapeDtypeStruct((length, 3 * width), BF),
            jax.ShapeDtypeStruct((2, width), F32),
        ),
        in_specs=[FAR] + [VMEM] * (3 + len(blocks)) + [ANYWHERE] * len(gates),
        out_specs=(VMEM, VMEM),
        scratch_shapes=[
            pltpu.VMEM((heads, length, length), BF),
            pltpu.VMEM((length, width), BF),
            pltpu.SemaphoreType.DMA((heads,)),
        ],
        compiler_params=PARAMS,
        cost_estimate=pl.CostEstimate(
            flops=10_000_000_000, bytes_accessed=10_000_000, transcendentals=0
        ),
    )(probability, queries, keys, values, *blocks, *gates)


def place_bit(bit):
    return (lax.axis_index("context") // bit) % 2 == 0


def halves_out(value, bit, own_ref, other_ref):
    rows = own_ref.shape[0]
    low = place_bit(bit)
    own_ref[...] = jnp.where(low, value[:rows], value[rows:])
    other_ref[...] = jnp.where(low, value[rows:], value[:rows]).astype(BF)


def pair_grad_kernel(left, left_pair, right, right_pair, _, own_ref, other_ref):
    value = product_left(left[...], right[...]) + product_left(left_pair[...], right_pair[...])
    halves_out(value, 1, own_ref, other_ref)


def pair_grad(left, left_pair, right, right_pair, gate):
    shape = (left.shape[1] // 2, right.shape[1])
    return pl.pallas_call(
        pair_grad_kernel,
        out_shape=(jax.ShapeDtypeStruct(shape, F32), jax.ShapeDtypeStruct(shape, BF)),
        in_specs=[VMEM] * 4 + [ANYWHERE],
        out_specs=(VMEM,) * 2,
        compiler_params=PARAMS,
    )(left, left_pair, right, right_pair, gate)


def column_grad_kernel(extra, left, right, *refs):
    mine_ref, sent_ref = refs[-2:]
    rows, step = left.shape[1], mine_ref.shape[1]
    sent_ref[:rows] = product_left(left[...], right[:, step:]).astype(BF)
    mine_ref[:rows] = product_left(left[...], right[:, :step])
    if extra:
        low = refs[0][...].astype(BF)
        sent_ref[rows:] = low
        mine_ref[rows:] = low.astype(F32)


def column_grad(left, right, gate, extra=None):
    rows = left.shape[1] + (0 if extra is None else extra.shape[0])
    shape = (rows, right.shape[1] // 2)
    more = [] if extra is None else [extra]
    return pl.pallas_call(
        functools.partial(column_grad_kernel, len(more)),
        out_shape=(jax.ShapeDtypeStruct(shape, F32), jax.ShapeDtypeStruct(shape, BF)),
        in_specs=[VMEM] * (2 + len(more)) + [ANYWHERE],
        out_specs=(VMEM,) * 2,
        compiler_params=PARAMS,
    )(left, right, *more, gate)


def sent_grad_kernel(left, right, sums, *refs):
    sent_ref = refs[-1]
    step = left.shape[1] // 2
    sent_ref[:step] = product_left(left[:, step:], right[...]).astype(BF)
    sent_ref[step:] = jnp.zeros_like(sent_ref[step:])
    sent_ref[step : step + 2, : sums.shape[1]] = sums[...].astype(BF)


def sent_grad(left, right, sums, gates):
    return pl.pallas_call(
        sent_grad_kernel,
        out_shape=jax.ShapeDtypeStruct((left.shape[1] // 2 + 16, right.shape[1]), BF),
        in_specs=[VMEM] * 3 + [ANYWHERE] * len(gates),
        out_specs=VMEM,
        compiler_params=PARAMS,
    )(left, right, sums, *gates)


def split_kernel(count, bit, *refs):
    value = refs[0][...].astype(F32)
    for other in refs[1:count]:
        value = value + other[...].astype(F32)
    halves_out(value, bit, *refs[-2:])


def split(values, bit, gates=()):
    shape = (values[0].shape[0] // 2, values[0].shape[1])
    return pl.pallas_call(
        functools.partial(split_kernel, len(values), bit),
        out_shape=(jax.ShapeDtypeStruct(shape, F32), jax.ShapeDtypeStruct(shape, BF)),
        in_specs=[VMEM] * len(values) + [ANYWHERE] * len(gates),
        out_specs=(VMEM,) * 2,
        compiler_params=PARAMS,
    )(*values, *gates)


def split_parts_kernel(parts, merged, bit, *refs):
    own_ref, other_ref = refs[-2:]
    low = place_bit(bit)
    start = 0
    for number, rows in enumerate(parts):
        if merged:
            value = refs[0][start : start + rows] + refs[1][start : start + rows].astype(F32)
        else:
            value = refs[2 * number][...] + refs[2 * number + 1][...].astype(F32)
        first, second = value[: rows // 2], value[rows // 2 :]
        at = slice(start // 2, (start + rows) // 2)
        own_ref[at] = jnp.where(low, first, second)
        other_ref[at] = jnp.where(low, second, first).astype(BF)
        start += rows


def split_parts(values, parts, bit, gates):
    merged = len(values) == 2
    shape = (sum(parts) // 2, values[0].shape[1])
    return pl.pallas_call(
        functools.partial(split_parts_kernel, parts, merged, bit),
        out_shape=(jax.ShapeDtypeStruct(shape, F32), jax.ShapeDtypeStruct(shape, BF)),
        in_specs=[VMEM] * len(values) + [ANYWHERE] * len(gates),
        out_specs=(VMEM,) * 2,
        compiler_params=PARAMS,
    )(*values, *gates)


def join_parts_kernel(parts, last, bit, own_ref, other_ref, *refs):
    low = place_bit(bit)
    start = 0
    for number, rows in enumerate(parts):
        at = slice(start, start + rows)
        own, other = own_ref[at], other_ref[at]
        ref, base = (refs[number], 0) if last else (refs[0], 2 * start)
        ref[base : base + rows] = jnp.where(low, own, other).astype(ref.dtype)
        ref[base + rows : base + 2 * rows] = jnp.where(low, other, own).astype(ref.dtype)
        start += rows


def join_parts(own, other, parts, bit, last):
    columns = own.shape[1]
    if last:
        shapes = tuple(jax.ShapeDtypeStruct((2 * rows, columns), F32) for rows in parts)
    else:
        shapes = (jax.ShapeDtypeStruct((2 * own.shape[0], columns), BF),)
    return pl.pallas_call(
        functools.partial(join_parts_kernel, parts, last, bit),
        out_shape=shapes,
        in_specs=[VMEM] * 2,
        out_specs=(VMEM,) * len(shapes),
        compiler_params=PARAMS,
    )(own, other)


def finish_kernel(parts, own_ref, other_ref, down_ref, out_ref, *small_refs):
    low = place_bit(1)
    joined = []
    start = 0
    for rows in parts:
        own, other = own_ref[start : start + rows], other_ref[start : start + rows]
        joined.append((jnp.where(low, own, other), jnp.where(low, other, own)))
        start += rows
    for number in range(2):
        down_ref[number * parts[0] : (number + 1) * parts[0]] = joined[0][number].astype(F32)
    value = jnp.concatenate([part.astype(F32) for part in joined[1]], axis=0)
    at = out_ref.shape[0]
    out_ref[...] = value[:at]
    step = value.shape[1]
    for ref in small_refs:
        for row in range(ref.shape[0]):
            for piece in range(ref.shape[1] // step):
                ref[row : row + 1, piece * step : (piece + 1) * step] = value[at : at + 1]
                at += 1


def finish(own, other, parts, out_rows, width, hidden):
    columns = own.shape[1]
    shapes = [(2 * parts[0], columns), (out_rows, columns)] + [(2, width)] * 3 + [(1, hidden)]
    return pl.pallas_call(
        functools.partial(finish_kernel, parts),
        out_shape=tuple(jax.ShapeDtypeStruct(shape, F32) for shape in shapes),
        in_specs=[VMEM] * 2,
        out_specs=(VMEM,) * len(shapes),
        compiler_params=PARAMS,
    )(own, other)


def add_wide_kernel(first_ref, second_ref, *refs):
    refs[-1][...] = first_ref[...].astype(F32) + second_ref[...].astype(F32)


def add_wide(first, second, gates):
    return pl.pallas_call(
        add_wide_kernel,
        out_shape=jax.ShapeDtypeStruct(first.shape, F32),
        in_specs=[VMEM] * 2 + [ANYWHERE] * len(gates),
        out_specs=VMEM,
        compiler_params=PARAMS,
    )(first, second, *gates)


def add_kernel(own_ref, other_ref, *refs):
    refs[-1][...] = (own_ref[...] + other_ref[...].astype(F32)).astype(BF)


def add_low(own, other, gates=()):
    return pl.pallas_call(
        add_kernel,
        out_shape=jax.ShapeDtypeStruct(own.shape, BF),
        in_specs=[VMEM] * 2 + [ANYWHERE] * len(gates),
        out_specs=VMEM,
        compiler_params=PARAMS,
    )(own, other, *gates)


def join_kernel(bit, own_ref, other_ref, *refs):
    rows = own_ref.shape[0]
    low = place_bit(bit)
    own, other = own_ref[...], other_ref[...]
    refs[-1][:rows] = jnp.where(low, own, other).astype(refs[-1].dtype)
    refs[-1][rows:] = jnp.where(low, other, own).astype(refs[-1].dtype)


def join(own, other, bit, dtype, gates=()):
    return pl.pallas_call(
        functools.partial(join_kernel, bit),
        out_shape=jax.ShapeDtypeStruct((2 * own.shape[0], own.shape[1]), dtype),
        in_specs=[VMEM] * 2 + [ANYWHERE] * len(gates),
        out_specs=VMEM,
        compiler_params=PARAMS,
    )(own, other, *gates)


def sums_kernel(one, two, first, normed_one, top, normed_two, _, out_ref):
    def put(row, value):
        out_ref[row : row + 1] = jnp.sum(value, axis=0, keepdims=True)

    put(0, one[...])
    put(1, two[...])
    put(2, first[...] * normed_one[...])
    put(3, top[...] * normed_two[...])
    put(4, first[...])
    put(5, top[...])


def row_sums(*operands):
    return pl.pallas_call(
        sums_kernel,
        out_shape=jax.ShapeDtypeStruct((6, operands[0].shape[1]), F32),
        in_specs=[VMEM] * 6 + [ANYWHERE],
        out_specs=VMEM,
        compiler_params=PARAMS,
    )(*operands)


def build(mesh):
    count = dict(mesh.shape)
    paired = count["weight"] == 2

    def flip(value, axis, bit):
        return lax.ppermute(value, axis, [(i, i ^ bit) for i in range(count[axis])])

    def bits(axis):
        bit, found = 1, []
        while bit < count[axis]:
            found.append(bit)
            bit *= 2
        return found

    def shards(
        tokens,
        segments,
        query_key_value_weight,
        input_bias,
        output_weight,
        row_bias,
        norm_gain,
        norm_bias,
        up_weight,
        up_bias,
        down_weight,
        cotangent,
    ):
        weight_at = lax.axis_index("weight")
        context_at = lax.axis_index("context")
        core_at = lax.axis_index("tensor") % 2
        rows, width = tokens.shape
        half = rows // 2
        shard_width = input_bias.shape[2]
        heads = shard_width // HD
        packs = count["context"]

        def columns(value):
            if not paired:
                return value
            middle = value.shape[-1] // 2
            swapped = jnp.concatenate([value[..., middle:], value[..., :middle]], axis=-1)
            return jnp.where(weight_at == 0, value, swapped)

        def own_rows(value):
            middle = value.shape[0] // 2
            swapped = jnp.concatenate([value[middle:], value[:middle]], axis=0)
            return jnp.where(core_at == 0, value, swapped)

        def swapped(value):
            return flip(value, "weight", 1)

        def gather_weight(value, axis):
            if paired:
                return [value, flip(value, "weight", 1)]
            return [lax.all_gather(value, "weight", axis=axis, tiled=True)]

        def contract(value, groups):
            step = width // len(groups)
            total = product(value[:, :step], groups[0])
            for number in range(1, len(groups)):
                total = total + product(
                    value[:, number * step : (number + 1) * step], groups[number]
                )
            return total

        def expand(value, groups):
            parts = [product(value, group) for group in groups]
            return parts[0] if len(parts) == 1 else jnp.concatenate(parts, axis=1)

        def contract_right(value, groups):
            step = width // len(groups)
            total = product_right(value[:, :step], groups[0])
            for number in range(1, len(groups)):
                total = total + product_right(
                    value[:, number * step : (number + 1) * step], groups[number]
                )
            return total

        def expand_right(value, groups):
            parts = [product_right(value, group) for group in groups]
            return parts[0] if len(parts) == 1 else jnp.concatenate(parts, axis=1)

        def row_total(partial, gates=()):
            mine, theirs = partial[:half], partial[half:].astype(BF)
            received = flip(theirs, "tensor", 1)
            total = add_wide(mine, received, gates) if gates else mine + received.astype(F32)
            for bit in bits("tensor")[1:-1]:
                low = total.astype(BF)
                total = low.astype(F32) + flip(low, "tensor", bit).astype(F32)
            low = total.astype(BF)
            return low, flip(low, "tensor", bits("tensor")[-1])

        def both_halves(value):
            return jnp.concatenate([value, flip(value, "tensor", 1)], axis=0)

        def take_half(value, which):
            middle = value.shape[0] // 2
            return lax.dynamic_slice_in_dim(value, which * middle, middle, axis=0)

        def context_total(value):
            return lax.psum(value.astype(BF), "context").astype(F32)

        def context_blocks(value):
            blocks = [value]
            for bit in reversed(bits("context")):
                blocks = blocks + [flip(block, "context", bit) for block in blocks]
            order = [0]
            for bit in reversed(bits("context")):
                order = order + [at ^ bit for at in order]
            return [blocks[order.index(j)] for j in range(packs)]

        def in_order(blocks):
            placed = []
            for at in range(packs):
                chosen = blocks[0]
                for j in range(1, packs):
                    chosen = jnp.where(context_at == (at ^ j), blocks[j], chosen)
                placed.append(chosen)
            return jnp.concatenate(placed, axis=0)

        gains, shifts, row_pair = columns(norm_gain[0]), columns(norm_bias[0]), columns(row_bias[0])
        cotangent_rows = columns(take_half(cotangent, core_at)).astype(F32)

        projection = query_key_value_weight[0].reshape(-1, 3 * shard_width)
        input_groups = gather_weight(projection, 0)

        def with_segments(which):
            numbers = take_half(segments, which).astype(BF)
            numbers = jnp.pad(numbers[None], ((0, 15), (0, width - half)))
            return jnp.concatenate([take_half(tokens, which), numbers], axis=0)

        halves = context_blocks(with_segments(core_at))
        up_groups = gather_weight(after(up_weight[0], halves[2 % packs]), 0)
        output_groups = gather_weight(after(output_weight[0], halves[2 % packs]), 1)
        down_groups = gather_weight(after(down_weight[0], halves[2 % packs]), 1)
        others = [with_segments(1 - core_at)]
        if packs == 4:
            tall = halves[1].shape[0]
            both = flip(jnp.concatenate(halves[1:3], axis=0), "tensor", 1)
            others += [both[:tall], both[tall:], flip(halves[3], "tensor", 1)]
        else:
            others += [flip(block, "tensor", 1) for block in halves[1:]]
        blocks = [block for pair in zip(halves, others) for block in pair]
        pack_queries, pack_keys, pack_values, context, pack_rows, pack_segments = front(
            blocks, input_bias[0], input_groups
        )

        def own_block(value):
            return lax.dynamic_slice_in_dim(value, context_at * rows, rows, 0)

        hidden_half = columns(take_half(tokens, core_at)).astype(F32)
        sent, received = row_total(expand(context, output_groups))
        pack_probability, token = probabilities(
            pack_queries, pack_keys, pack_segments, (sent, up_groups[-1])
        )
        attended = add_wide(sent, received, (token, down_groups[-1])) + row_pair[0]
        normed_one, inverse_one = normalize(hidden_half + attended)
        first_norm = normed_one * gains[0] + shifts[0]
        first_low = both_halves(first_norm.astype(BF))

        preactivation = contract(first_low, up_groups) + up_bias[0]
        cumulative = 0.5 * (1.0 + lax.erf(preactivation * ROOT_HALF))
        activated = (preactivation * cumulative).astype(BF)
        slope = cumulative + preactivation * DENSITY_FACTOR * jnp.exp(
            -0.5 * preactivation * preactivation
        )
        sent, received = row_total(expand(activated, down_groups))
        step = width // 2
        gates = ()
        if paired:
            first_pair = swapped(first_low[:, step:])
            gates = (first_pair,)
        total = add_wide(sent, received, gates)
        normed_two, inverse_two = normalize(first_norm + (total + row_pair[1]))
        result = (normed_two * gains[1] + shifts[1]).astype(BF)

        layer_output = columns(own_rows(both_halves(result)))
        grad_two = normalize_back(cotangent_rows, normed_two, inverse_two, gains[1])
        grad_two_low = both_halves(grad_two.astype(BF))

        def shares(left, right, axis):
            step = width // 2
            if axis == 0:
                return (
                    product_left(left[:, :step], right),
                    product_left(left[:, step:], right).astype(BF),
                )
            return (
                product_left(left, right[:, :step]),
                product_left(left, right[:, step:]).astype(BF),
            )

        def scattered(left, right, axis):
            return lax.psum_scatter(
                product_left(left, right).astype(BF), "weight", scatter_dimension=axis, tiled=True
            ).astype(F32)

        grad_pre = contract_right(grad_two_low, down_groups) * slope
        grad_pre_low = grad_pre.astype(BF)
        sent, received = row_total(expand_right(grad_pre_low, up_groups))
        gates = ()
        if paired:
            pre_pair = swapped(grad_pre_low)
            down_mine, down_sent = column_grad(activated, grad_two_low, sent)
            down_received = swapped(down_sent)
            gates = (down_sent, pre_pair)
            up_halves = pair_grad(first_low[:, :step], first_pair, grad_pre_low, pre_pair, sent)
        grad_first = grad_two + add_wide(sent, received, gates)
        grad_one = normalize_back(grad_first, normed_one, inverse_one, gains[0])
        grad_one_low = both_halves(grad_one.astype(BF))
        grad_context = contract_right(grad_one_low, output_groups).astype(BF)
        grad_context_blocks = context_blocks(grad_context)

        small = row_sums(
            grad_one, grad_two, grad_first, normed_one, cotangent_rows, normed_two, grad_context
        )
        small = small + flip(small, "tensor", 1)
        share_width = output_weight.shape[2]
        joined = jnp.concatenate([columns(small).reshape(-1), jnp.sum(grad_pre, axis=0)])
        size = joined.shape[0]
        joined = jnp.pad(joined, (0, -size % (16 * share_width))).reshape(-1, share_width)
        out_rows, joined_rows = context.shape[1], joined.shape[0]
        chained = paired and packs == 4
        gates = []
        if chained:
            up_halves = split(
                [up_halves[0], flip(up_halves[1], "context", 1)], 2, (grad_context_blocks[2],)
            )
            last = (grad_context_blocks[-1],)
            below = -out_rows % 256
            joined = jnp.pad(joined, ((0, below - joined_rows), (0, 0)))
            out_mine, out_sent = column_grad(context, grad_one_low, grad_context, joined)
            parts = (down_mine.shape[0], out_mine.shape[0])
            halves = split_parts(
                (down_mine, down_received, out_mine, swapped(out_sent)), parts, 1, last
            )
            gates = [halves[1], up_halves[1], layer_output]

        pack_projected, bias_grads = attention_back(
            pltpu.with_memory_space_constraint(pack_probability, pltpu.HBM),
            pack_queries,
            pack_keys,
            pack_values,
            grad_context_blocks,
            gates,
        )
        ends = ()
        if chained:
            parts = tuple(rows // 2 for rows in parts)
            halves = split_parts(
                (halves[0], flip(halves[1], "context", 1)), parts, 2, (pack_projected,)
            )
            ends = (up_halves[1], halves[1])
            input_sent = sent_grad(
                pack_rows, pack_projected, bias_grads, (up_halves[1], halves[1])
            )
            low = add_low(up_halves[0], flip(up_halves[1], "context", 2))
            low = join(low, flip(low, "context", 2), 2, BF)
            grad_up = join(low, flip(low, "context", 1), 1, F32)
            low = add_low(halves[0], flip(halves[1], "context", 2))
            small_parts = tuple(rows // 2 for rows in parts)
            (low,) = join_parts(low, flip(low, "context", 2), small_parts, 2, False)
            grad_down, grad_out, *small, hidden_sum = finish(
                low, flip(low, "context", 1), parts, out_rows, width, up_bias.shape[1]
            )
            received = swapped(input_sent)
            grad_input = product_left(pack_rows[:, :step], pack_projected) + received[
                :step
            ].astype(F32)
            bias_grads = bias_grads.astype(BF).astype(F32) + received[
                step : step + 2, :shard_width
            ].astype(F32)
        else:
            grad_input = scattered(pack_rows, pack_projected, 0)
            bias_grads = lax.psum(bias_grads, "weight")
            grad_down = context_total(scattered(activated, grad_two_low, 1))
            grad_up = context_total(scattered(first_low, grad_pre_low, 0))
            grad_out = context_total(scattered(context, grad_one_low, 1))
            joined = lax.psum(lax.psum(joined, "weight"), "context").reshape(-1)
            small = joined[: 6 * width].reshape(3, 2, width)
            hidden_sum = joined[None, 6 * width : size]
        sent, received = row_total(expand_right(own_block(pack_projected), input_groups), ends)
        total = sent.astype(F32) + received.astype(F32)
        grad_tokens = columns(own_rows(both_halves(grad_one + total)))
        return (
            layer_output,
            grad_tokens,
            grad_input.reshape(1, -1, 3, shard_width),
            bias_grads[None],
            grad_out[None],
            small[0][None],
            small[1][None],
            small[2][None],
            grad_up[None],
            hidden_sum,
            grad_down[None],
        )

    return shards


def solution(mesh):
    token_rows = P(("weight", "context"), None)
    input_spec = P(None, "weight", None, "tensor")
    out_spec = P(None, "tensor", "weight")
    placed = (
        token_rows,
        P(("weight", "context")),
        input_spec,
        P(None, None, "tensor"),
        out_spec,
        P(),
        P(),
        P(),
        P(None, "weight", "tensor"),
        P(None, "tensor"),
        out_spec,
        token_rows,
    )
    return jax.shard_map(
        build(mesh),
        mesh=mesh,
        in_specs=placed,
        out_specs=(
            token_rows,
            token_rows,
            input_spec,
            P(None, None, "tensor"),
            out_spec,
            P(),
            P(),
            P(),
            P(None, "weight", "tensor"),
            P(None, "tensor"),
            out_spec,
        ),
        check_vma=False,
    )
```

```python
import functools

import jax
import jax.experimental.pallas as pl
import jax.experimental.pallas.tpu as pltpu
import jax.numpy as jnp
from jax import lax
from jax.sharding import PartitionSpec as P

HD = 64
EPSILON = 1e-05
NEG_FILL = -1e30
ROOT_HALF = 0.7071067811865476
DENSITY_FACTOR = 0.3989422804014327
BF = jnp.bfloat16
F32 = jnp.float32


def product(left, right):
    return jnp.dot(left, right, preferred_element_type=F32)


def product_left(left, right):
    return lax.dot_general(left, right, (((0,), (0,)), ((), ())), preferred_element_type=F32)


def product_right(left, right):
    return lax.dot_general(left, right, (((1,), (1,)), ((), ())), preferred_element_type=F32)


def normalize(summed):
    center = summed - jnp.mean(summed, axis=-1, keepdims=True)
    inverse = lax.rsqrt(jnp.mean(center * center, axis=-1, keepdims=True) + EPSILON)
    return center * inverse, inverse


def normalize_back(grad_output, normed, inverse, gain_vector):
    scaled = grad_output * gain_vector
    return inverse * (
        scaled
        - jnp.mean(scaled, axis=-1, keepdims=True)
        - normed * jnp.mean(scaled * normed, axis=-1, keepdims=True)
    )


VMEM = pl.BlockSpec(memory_space=pltpu.VMEM)
FAR = pl.BlockSpec(memory_space=pltpu.HBM)
ANYWHERE = pl.BlockSpec(memory_space=pl.ANY)
PARAMS = pltpu.CompilerParams(vmem_limit_bytes=40 * 1024 * 1024)


def after(value, *others):
    zero = jnp.zeros((), F32)
    for other in others:
        first = lax.slice(other, (0,) * other.ndim, (1,) * other.ndim).reshape(())
        zero = zero + jnp.minimum(jnp.abs(first.astype(F32)), 0.0)
    return value + zero.astype(value.dtype)


def softmax_block(keys, queries, same):
    scores = jnp.where(same, product_right(keys, queries) * HD**-0.5, NEG_FILL)
    exponent = jnp.exp(scores - jnp.max(scores, axis=0, keepdims=True))
    total = jnp.sum(exponent, axis=0, keepdims=True)
    return (exponent * (1.0 / total)).astype(BF)


def as_column(row):
    return jnp.broadcast_to(row, (8, row.shape[1])).T[:, :1]


def block_start(number, rows):
    return pl.multiple_of((lax.axis_index("context") ^ number) * rows, rows)


def front_kernel(heads, packs, paired, *refs):
    blocks, refs = refs[: 2 * packs], refs[2 * packs :]
    groups = 2 if paired else 1
    b_ref, weights, refs = refs[0], refs[1 : 1 + groups], refs[1 + groups :]
    q_ref, k_ref, v_ref, c_ref, x_ref, row_ref = refs
    width = heads * HD
    model = x_ref.shape[1]
    rows = c_ref.shape[0]
    half = rows // 2
    step = model // groups
    for number in range(packs):
        for which in range(2):
            block = blocks[2 * number + which]
            at = pl.multiple_of(block_start(number, rows) + which * half, half)
            if paired:
                first = lax.axis_index("weight") == 0
                left, right = block[:half, :step], block[:half, step:]
                x_ref[pl.ds(at, half), :step] = jnp.where(first, left, right)
                x_ref[pl.ds(at, half), step:] = jnp.where(first, right, left)
            else:
                x_ref[pl.ds(at, half)] = block[:half]
            row_ref[:, pl.ds(at, half)] = block[half : half + 16, :half].astype(F32)[:1]
    for number, (out_ref, bias) in enumerate(((q_ref, 0), (k_ref, None), (v_ref, 1))):
        total = None
        for group in range(groups):
            part = product(
                x_ref[:, group * step : (group + 1) * step],
                weights[group][:, number * width : (number + 1) * width],
            )
            total = part if total is None else total + part
        if bias is not None:
            total = total + b_ref[bias : bias + 1]
        out_ref[...] = total.astype(BF)
    at = block_start(0, rows)
    same = as_column(row_ref[...]) == row_ref[:, pl.ds(at, rows)]
    for head in range(heads):
        lanes = slice(head * HD, (head + 1) * HD)
        probability = softmax_block(k_ref[:, lanes], q_ref[pl.ds(at, rows), lanes], same)
        c_ref[:, lanes] = product(v_ref[:, lanes].T, probability).T.astype(BF)


def front(blocks, biases, groups):
    packs = len(blocks) // 2
    rows = 2 * (blocks[0].shape[0] - 16)
    model = blocks[0].shape[1]
    width = biases.shape[1]
    whole = jax.ShapeDtypeStruct((packs * rows, width), BF)
    return pl.pallas_call(
        functools.partial(front_kernel, width // HD, packs, len(groups) == 2),
        out_shape=(
            whole,
            whole,
            whole,
            jax.ShapeDtypeStruct((rows, width), BF),
            jax.ShapeDtypeStruct((packs * rows, model), BF),
            jax.ShapeDtypeStruct((1, packs * rows), F32),
        ),
        in_specs=[VMEM] * (2 * packs + 1 + len(groups)),
        out_specs=(VMEM,) * 6,
        compiler_params=PARAMS,
    )(*blocks, biases, *groups)


def probability_kernel(heads, block, q_ref, k_ref, row_ref, *refs):
    a_hbm, token_ref, a_ref, copy_sems = refs[-4:]
    token_ref[...] = jnp.minimum(jnp.abs(row_ref[:, : token_ref.shape[1]]), 0.0)
    count = q_ref.shape[0] // block

    def copy(number):
        at = pl.multiple_of(number * block, block)
        return pltpu.make_async_copy(
            a_ref.at[:, :, pl.ds(at, block)],
            a_hbm.at[:, :, pl.ds(at, block)],
            copy_sems.at[number],
        )

    def body(number, carry):
        at = pl.multiple_of(number * block, block)
        same = as_column(row_ref[...]) == row_ref[:, pl.ds(at, block)]
        for head in range(heads):
            lanes = slice(head * HD, (head + 1) * HD)
            a_ref[head, :, pl.ds(at, block)] = softmax_block(
                k_ref[:, lanes], q_ref[pl.ds(at, block), lanes], same
            )
        copy(number).start()
        return carry

    lax.fori_loop(0, count, body, 0)
    for number in range(count):
        copy(number).wait()


def probabilities(queries, keys, segments, gates):
    length, width = queries.shape
    heads = width // HD
    block = 256
    return pl.pallas_call(
        functools.partial(probability_kernel, heads, block),
        out_shape=(
            pltpu.HBM((heads, length, length), BF),
            jax.ShapeDtypeStruct((1, 128), F32),
        ),
        in_specs=[VMEM] * 3 + [ANYWHERE] * len(gates),
        out_specs=(FAR, VMEM),
        scratch_shapes=[
            pltpu.VMEM((heads, length, length), BF),
            pltpu.SemaphoreType.DMA((length // block,)),
        ],
        compiler_params=PARAMS,
    )(queries, keys, segments, *gates)


def attention_back_kernel(heads, packs, a_hbm, q_ref, k_ref, v_ref, *refs):
    blocks, (p_ref, b_ref, a_ref, c_ref, copy_sems) = refs[:packs], refs[-5:]
    width = heads * HD
    scale = jnp.asarray(HD**-0.5, BF)
    copies = [
        pltpu.make_async_copy(a_hbm.at[head], a_ref.at[head], copy_sems.at[head])
        for head in range(heads)
    ]
    for copy in copies:
        copy.start()
    for number, block in enumerate(blocks):
        rows = block.shape[0]
        c_ref[pl.ds(block_start(number, rows), rows)] = block[...]
    for head in range(heads):
        lanes = slice(head * HD, (head + 1) * HD)
        grad_context = c_ref[:, lanes]
        copies[head].wait()
        low = a_ref[head]
        wide = low.astype(F32)
        weighted = wide * product_right(v_ref[:, lanes], grad_context)
        row_dot = jnp.sum(weighted, axis=0, keepdims=True)
        grad_scores = (weighted - wide * row_dot).astype(BF)
        grad_values = product(low, grad_context)
        grad_keys = product(grad_scores, q_ref[:, lanes] * scale)
        grad_queries = product((k_ref[:, lanes] * scale).T, grad_scores).T
        p_ref[:, lanes] = grad_queries.astype(BF)
        p_ref[:, width + head * HD : width + (head + 1) * HD] = grad_keys.astype(BF)
        p_ref[:, 2 * width + head * HD : 2 * width + (head + 1) * HD] = grad_values.astype(BF)
        b_ref[0:1, lanes] = jnp.sum(grad_queries, axis=0, keepdims=True)
        b_ref[1:2, lanes] = jnp.sum(grad_values, axis=0, keepdims=True)


def attention_back(probability, queries, keys, values, blocks, gates):
    length, width = queries.shape
    heads = width // HD
    return pl.pallas_call(
        functools.partial(attention_back_kernel, heads, len(blocks)),
        out_shape=(
            jax.ShapeDtypeStruct((length, 3 * width), BF),
            jax.ShapeDtypeStruct((2, width), F32),
        ),
        in_specs=[FAR] + [VMEM] * (3 + len(blocks)) + [ANYWHERE] * len(gates),
        out_specs=(VMEM, VMEM),
        scratch_shapes=[
            pltpu.VMEM((heads, length, length), BF),
            pltpu.VMEM((length, width), BF),
            pltpu.SemaphoreType.DMA((heads,)),
        ],
        compiler_params=PARAMS,
        cost_estimate=pl.CostEstimate(
            flops=10_000_000_000, bytes_accessed=10_000_000, transcendentals=0
        ),
    )(probability, queries, keys, values, *blocks, *gates)


def place_bit(bit):
    return (lax.axis_index("context") // bit) % 2 == 0


def halves_out(value, bit, own_ref, other_ref):
    rows = own_ref.shape[0]
    low = place_bit(bit)
    own_ref[...] = jnp.where(low, value[:rows], value[rows:])
    other_ref[...] = jnp.where(low, value[rows:], value[:rows]).astype(BF)


def pair_grad_kernel(left, left_pair, right, right_pair, _, own_ref, other_ref):
    value = product_left(left[...], right[...]) + product_left(left_pair[...], right_pair[...])
    halves_out(value, 1, own_ref, other_ref)


def pair_grad(left, left_pair, right, right_pair, gate):
    shape = (left.shape[1] // 2, right.shape[1])
    return pl.pallas_call(
        pair_grad_kernel,
        out_shape=(jax.ShapeDtypeStruct(shape, F32), jax.ShapeDtypeStruct(shape, BF)),
        in_specs=[VMEM] * 4 + [ANYWHERE],
        out_specs=(VMEM,) * 2,
        compiler_params=PARAMS,
    )(left, left_pair, right, right_pair, gate)


def column_grad_kernel(extra, left, right, *refs):
    mine_ref, sent_ref = refs[-2:]
    rows, step = left.shape[1], mine_ref.shape[1]
    sent_ref[:rows] = product_left(left[...], right[:, step:]).astype(BF)
    mine_ref[:rows] = product_left(left[...], right[:, :step])
    if extra:
        low = refs[0][...].astype(BF)
        sent_ref[rows:] = low
        mine_ref[rows:] = low.astype(F32)


def column_grad(left, right, gate, extra=None):
    rows = left.shape[1] + (0 if extra is None else extra.shape[0])
    shape = (rows, right.shape[1] // 2)
    more = [] if extra is None else [extra]
    return pl.pallas_call(
        functools.partial(column_grad_kernel, len(more)),
        out_shape=(jax.ShapeDtypeStruct(shape, F32), jax.ShapeDtypeStruct(shape, BF)),
        in_specs=[VMEM] * (2 + len(more)) + [ANYWHERE],
        out_specs=(VMEM,) * 2,
        compiler_params=PARAMS,
    )(left, right, *more, gate)


def sent_grad_kernel(left, right, sums, *refs):
    sent_ref = refs[-1]
    step = left.shape[1] // 2
    sent_ref[:step] = product_left(left[:, step:], right[...]).astype(BF)
    below = jnp.concatenate([sums[...], jnp.zeros((14, sums.shape[1]), F32)], axis=0)
    sent_ref[step:] = jnp.zeros_like(sent_ref[step:])
    sent_ref[step:, : sums.shape[1]] = below.astype(BF)


def sent_grad(left, right, sums, gates):
    return pl.pallas_call(
        sent_grad_kernel,
        out_shape=jax.ShapeDtypeStruct((left.shape[1] // 2 + 16, right.shape[1]), BF),
        in_specs=[VMEM] * 3 + [ANYWHERE] * len(gates),
        out_specs=VMEM,
        compiler_params=PARAMS,
    )(left, right, sums, *gates)


def split_kernel(count, bit, *refs):
    value = refs[0][...].astype(F32)
    for other in refs[1:count]:
        value = value + other[...].astype(F32)
    halves_out(value, bit, *refs[-2:])


def split(values, bit, gates=()):
    shape = (values[0].shape[0] // 2, values[0].shape[1])
    return pl.pallas_call(
        functools.partial(split_kernel, len(values), bit),
        out_shape=(jax.ShapeDtypeStruct(shape, F32), jax.ShapeDtypeStruct(shape, BF)),
        in_specs=[VMEM] * len(values) + [ANYWHERE] * len(gates),
        out_specs=(VMEM,) * 2,
        compiler_params=PARAMS,
    )(*values, *gates)


def split_parts_kernel(parts, merged, bit, *refs):
    own_ref, other_ref = refs[-2:]
    low = place_bit(bit)
    start = 0
    for number, rows in enumerate(parts):
        if merged:
            value = refs[0][start : start + rows] + refs[1][start : start + rows].astype(F32)
        else:
            value = refs[2 * number][...] + refs[2 * number + 1][...].astype(F32)
        first, second = value[: rows // 2], value[rows // 2 :]
        at = slice(start // 2, (start + rows) // 2)
        own_ref[at] = jnp.where(low, first, second)
        other_ref[at] = jnp.where(low, second, first).astype(BF)
        start += rows


def split_parts(values, parts, bit, gates):
    merged = len(values) == 2
    shape = (sum(parts) // 2, values[0].shape[1])
    return pl.pallas_call(
        functools.partial(split_parts_kernel, parts, merged, bit),
        out_shape=(jax.ShapeDtypeStruct(shape, F32), jax.ShapeDtypeStruct(shape, BF)),
        in_specs=[VMEM] * len(values) + [ANYWHERE] * len(gates),
        out_specs=(VMEM,) * 2,
        compiler_params=PARAMS,
    )(*values, *gates)


def join_parts_kernel(parts, last, bit, own_ref, other_ref, *refs):
    low = place_bit(bit)
    start = 0
    for number, rows in enumerate(parts):
        at = slice(start, start + rows)
        own, other = own_ref[at], other_ref[at]
        ref, base = (refs[number], 0) if last else (refs[0], 2 * start)
        ref[base : base + rows] = jnp.where(low, own, other).astype(ref.dtype)
        ref[base + rows : base + 2 * rows] = jnp.where(low, other, own).astype(ref.dtype)
        start += rows


def join_parts(own, other, parts, bit, last):
    columns = own.shape[1]
    if last:
        shapes = tuple(jax.ShapeDtypeStruct((2 * rows, columns), F32) for rows in parts)
    else:
        shapes = (jax.ShapeDtypeStruct((2 * own.shape[0], columns), BF),)
    return pl.pallas_call(
        functools.partial(join_parts_kernel, parts, last, bit),
        out_shape=shapes,
        in_specs=[VMEM] * 2,
        out_specs=(VMEM,) * len(shapes),
        compiler_params=PARAMS,
    )(own, other)


def finish_kernel(parts, own_ref, other_ref, down_ref, out_ref, *small_refs):
    low = place_bit(1)
    joined = []
    start = 0
    for rows in parts:
        own, other = own_ref[start : start + rows], other_ref[start : start + rows]
        joined.append((jnp.where(low, own, other), jnp.where(low, other, own)))
        start += rows
    for number in range(2):
        down_ref[number * parts[0] : (number + 1) * parts[0]] = joined[0][number].astype(F32)
    value = jnp.concatenate([part.astype(F32) for part in joined[1]], axis=0)
    at = out_ref.shape[0]
    out_ref[...] = value[:at]
    step = value.shape[1]
    for ref in small_refs:
        for row in range(ref.shape[0]):
            for piece in range(ref.shape[1] // step):
                ref[row : row + 1, piece * step : (piece + 1) * step] = value[at : at + 1]
                at += 1


def finish(own, other, parts, out_rows, width, hidden):
    columns = own.shape[1]
    shapes = [(2 * parts[0], columns), (out_rows, columns)] + [(2, width)] * 3 + [(1, hidden)]
    return pl.pallas_call(
        functools.partial(finish_kernel, parts),
        out_shape=tuple(jax.ShapeDtypeStruct(shape, F32) for shape in shapes),
        in_specs=[VMEM] * 2,
        out_specs=(VMEM,) * len(shapes),
        compiler_params=PARAMS,
    )(own, other)


def add_wide_kernel(first_ref, second_ref, *refs):
    refs[-1][...] = first_ref[...].astype(F32) + second_ref[...].astype(F32)


def add_wide(first, second, gates):
    return pl.pallas_call(
        add_wide_kernel,
        out_shape=jax.ShapeDtypeStruct(first.shape, F32),
        in_specs=[VMEM] * 2 + [ANYWHERE] * len(gates),
        out_specs=VMEM,
        compiler_params=PARAMS,
    )(first, second, *gates)


def add_kernel(own_ref, other_ref, *refs):
    refs[-1][...] = (own_ref[...] + other_ref[...].astype(F32)).astype(BF)


def add_low(own, other, gates=()):
    return pl.pallas_call(
        add_kernel,
        out_shape=jax.ShapeDtypeStruct(own.shape, BF),
        in_specs=[VMEM] * 2 + [ANYWHERE] * len(gates),
        out_specs=VMEM,
        compiler_params=PARAMS,
    )(own, other, *gates)


def join_kernel(bit, own_ref, other_ref, *refs):
    rows = own_ref.shape[0]
    low = place_bit(bit)
    own, other = own_ref[...], other_ref[...]
    refs[-1][:rows] = jnp.where(low, own, other).astype(refs[-1].dtype)
    refs[-1][rows:] = jnp.where(low, other, own).astype(refs[-1].dtype)


def join(own, other, bit, dtype, gates=()):
    return pl.pallas_call(
        functools.partial(join_kernel, bit),
        out_shape=jax.ShapeDtypeStruct((2 * own.shape[0], own.shape[1]), dtype),
        in_specs=[VMEM] * 2 + [ANYWHERE] * len(gates),
        out_specs=VMEM,
        compiler_params=PARAMS,
    )(own, other, *gates)


def sums_kernel(one, two, first, normed_one, top, normed_two, _, out_ref):
    def put(row, value):
        out_ref[row : row + 1] = jnp.sum(value, axis=0, keepdims=True)

    put(0, one[...])
    put(1, two[...])
    put(2, first[...] * normed_one[...])
    put(3, top[...] * normed_two[...])
    put(4, first[...])
    put(5, top[...])


def row_sums(*operands):
    return pl.pallas_call(
        sums_kernel,
        out_shape=jax.ShapeDtypeStruct((6, operands[0].shape[1]), F32),
        in_specs=[VMEM] * 6 + [ANYWHERE],
        out_specs=VMEM,
        compiler_params=PARAMS,
    )(*operands)


def build(mesh):
    count = dict(mesh.shape)
    paired = count["weight"] == 2

    def flip(value, axis, bit):
        return lax.ppermute(value, axis, [(i, i ^ bit) for i in range(count[axis])])

    def bits(axis):
        bit, found = 1, []
        while bit < count[axis]:
            found.append(bit)
            bit *= 2
        return found

    def shards(
        tokens,
        segments,
        query_key_value_weight,
        input_bias,
        output_weight,
        row_bias,
        norm_gain,
        norm_bias,
        up_weight,
        up_bias,
        down_weight,
        cotangent,
    ):
        weight_at = lax.axis_index("weight")
        context_at = lax.axis_index("context")
        core_at = lax.axis_index("tensor") % 2
        rows, width = tokens.shape
        half = rows // 2
        shard_width = input_bias.shape[2]
        heads = shard_width // HD
        packs = count["context"]

        def columns(value):
            if not paired:
                return value
            middle = value.shape[-1] // 2
            swapped = jnp.concatenate([value[..., middle:], value[..., :middle]], axis=-1)
            return jnp.where(weight_at == 0, value, swapped)

        def own_rows(value):
            middle = value.shape[0] // 2
            swapped = jnp.concatenate([value[middle:], value[:middle]], axis=0)
            return jnp.where(core_at == 0, value, swapped)

        def swapped(value):
            return flip(value, "weight", 1)

        def gather_weight(value, axis):
            if paired:
                return [value, flip(value, "weight", 1)]
            return [lax.all_gather(value, "weight", axis=axis, tiled=True)]

        def contract(value, groups):
            step = width // len(groups)
            total = product(value[:, :step], groups[0])
            for number in range(1, len(groups)):
                total = total + product(
                    value[:, number * step : (number + 1) * step], groups[number]
                )
            return total

        def expand(value, groups):
            parts = [product(value, group) for group in groups]
            return parts[0] if len(parts) == 1 else jnp.concatenate(parts, axis=1)

        def contract_right(value, groups):
            step = width // len(groups)
            total = product_right(value[:, :step], groups[0])
            for number in range(1, len(groups)):
                total = total + product_right(
                    value[:, number * step : (number + 1) * step], groups[number]
                )
            return total

        def expand_right(value, groups):
            parts = [product_right(value, group) for group in groups]
            return parts[0] if len(parts) == 1 else jnp.concatenate(parts, axis=1)

        def row_total(partial, gates=()):
            mine, theirs = partial[:half], partial[half:].astype(BF)
            received = flip(theirs, "tensor", 1)
            total = add_wide(mine, received, gates) if gates else mine + received.astype(F32)
            for bit in bits("tensor")[1:-1]:
                low = total.astype(BF)
                total = low.astype(F32) + flip(low, "tensor", bit).astype(F32)
            low = total.astype(BF)
            return low, flip(low, "tensor", bits("tensor")[-1])

        def both_halves(value):
            return jnp.concatenate([value, flip(value, "tensor", 1)], axis=0)

        def take_half(value, which):
            middle = value.shape[0] // 2
            return lax.dynamic_slice_in_dim(value, which * middle, middle, axis=0)

        def context_total(value):
            return lax.psum(value.astype(BF), "context").astype(F32)

        def context_blocks(value):
            blocks = [value]
            for bit in reversed(bits("context")):
                blocks = blocks + [flip(block, "context", bit) for block in blocks]
            order = [0]
            for bit in reversed(bits("context")):
                order = order + [at ^ bit for at in order]
            return [blocks[order.index(j)] for j in range(packs)]

        def in_order(blocks):
            placed = []
            for at in range(packs):
                chosen = blocks[0]
                for j in range(1, packs):
                    chosen = jnp.where(context_at == (at ^ j), blocks[j], chosen)
                placed.append(chosen)
            return jnp.concatenate(placed, axis=0)

        gains, shifts, row_pair = columns(norm_gain[0]), columns(norm_bias[0]), columns(row_bias[0])
        cotangent_rows = columns(take_half(cotangent, core_at)).astype(F32)

        projection = query_key_value_weight[0].reshape(-1, 3 * shard_width)
        input_groups = gather_weight(projection, 0)

        def with_segments(which):
            numbers = take_half(segments, which).astype(BF)
            numbers = jnp.pad(numbers[None], ((0, 15), (0, width - half)))
            return jnp.concatenate([take_half(tokens, which), numbers], axis=0)

        halves = context_blocks(with_segments(core_at))
        up_groups = gather_weight(after(up_weight[0], halves[2 % packs]), 0)
        output_groups = gather_weight(after(output_weight[0], halves[2 % packs]), 1)
        down_groups = gather_weight(after(down_weight[0], halves[2 % packs]), 1)
        others = [with_segments(1 - core_at)]
        if packs == 4:
            tall = halves[1].shape[0]
            both = flip(jnp.concatenate(halves[1:3], axis=0), "tensor", 1)
            others += [both[:tall], both[tall:], flip(halves[3], "tensor", 1)]
        else:
            others += [flip(block, "tensor", 1) for block in halves[1:]]
        blocks = [block for pair in zip(halves, others) for block in pair]
        pack_queries, pack_keys, pack_values, context, pack_rows, pack_segments = front(
            blocks, input_bias[0], input_groups
        )

        def own_block(value):
            return lax.dynamic_slice_in_dim(value, context_at * rows, rows, 0)

        hidden_half = columns(take_half(tokens, core_at)).astype(F32)
        sent, received = row_total(expand(context, output_groups))
        pack_probability, token = probabilities(
            pack_queries, pack_keys, pack_segments, (sent, up_groups[-1])
        )
        attended = add_wide(sent, received, (token, down_groups[-1])) + row_pair[0]
        normed_one, inverse_one = normalize(hidden_half + attended)
        first_norm = normed_one * gains[0] + shifts[0]
        first_low = both_halves(first_norm.astype(BF))

        preactivation = contract(first_low, up_groups) + up_bias[0]
        cumulative = 0.5 * (1.0 + lax.erf(preactivation * ROOT_HALF))
        activated = (preactivation * cumulative).astype(BF)
        slope = cumulative + preactivation * DENSITY_FACTOR * jnp.exp(
            -0.5 * preactivation * preactivation
        )
        sent, received = row_total(expand(activated, down_groups))
        step = width // 2
        gates = ()
        if paired:
            first_pair = swapped(first_low[:, step:])
            gates = (first_pair,)
        total = add_wide(sent, received, gates)
        normed_two, inverse_two = normalize(first_norm + (total + row_pair[1]))
        result = (normed_two * gains[1] + shifts[1]).astype(BF)

        layer_output = columns(own_rows(both_halves(result)))
        grad_two = normalize_back(cotangent_rows, normed_two, inverse_two, gains[1])
        grad_two_low = both_halves(grad_two.astype(BF))

        def shares(left, right, axis):
            step = width // 2
            if axis == 0:
                return (
                    product_left(left[:, :step], right),
                    product_left(left[:, step:], right).astype(BF),
                )
            return (
                product_left(left, right[:, :step]),
                product_left(left, right[:, step:]).astype(BF),
            )

        def scattered(left, right, axis):
            return lax.psum_scatter(
                product_left(left, right).astype(BF), "weight", scatter_dimension=axis, tiled=True
            ).astype(F32)

        grad_pre = contract_right(grad_two_low, down_groups) * slope
        grad_pre_low = grad_pre.astype(BF)
        sent, received = row_total(expand_right(grad_pre_low, up_groups))
        gates = ()
        if paired:
            pre_pair = swapped(grad_pre_low)
            down_mine, down_sent = column_grad(activated, grad_two_low, sent)
            down_received = swapped(down_sent)
            gates = (down_sent, pre_pair)
            up_halves = pair_grad(first_low[:, :step], first_pair, grad_pre_low, pre_pair, sent)
        grad_first = grad_two + add_wide(sent, received, gates)
        grad_one = normalize_back(grad_first, normed_one, inverse_one, gains[0])
        grad_one_low = both_halves(grad_one.astype(BF))
        grad_context = contract_right(grad_one_low, output_groups).astype(BF)
        grad_context_blocks = context_blocks(grad_context)

        small = row_sums(
            grad_one, grad_two, grad_first, normed_one, cotangent_rows, normed_two, grad_context
        )
        small = small + flip(small, "tensor", 1)
        share_width = output_weight.shape[2]
        joined = jnp.concatenate([columns(small).reshape(-1), jnp.sum(grad_pre, axis=0)])
        size = joined.shape[0]
        joined = jnp.pad(joined, (0, -size % (16 * share_width))).reshape(-1, share_width)
        out_rows, joined_rows = context.shape[1], joined.shape[0]
        chained = paired and packs == 4
        gates = []
        if chained:
            up_halves = split(
                [up_halves[0], flip(up_halves[1], "context", 1)], 2, (grad_context_blocks[2],)
            )
            last = (grad_context_blocks[-1],)
            below = -out_rows % 256
            joined = jnp.pad(joined, ((0, below - joined_rows), (0, 0)))
            out_mine, out_sent = column_grad(context, grad_one_low, grad_context, joined)
            parts = (down_mine.shape[0], out_mine.shape[0])
            halves = split_parts(
                (down_mine, down_received, out_mine, swapped(out_sent)), parts, 1, last
            )
            gates = [halves[1], up_halves[1], layer_output]

        pack_projected, bias_grads = attention_back(
            pltpu.with_memory_space_constraint(pack_probability, pltpu.HBM),
            pack_queries,
            pack_keys,
            pack_values,
            grad_context_blocks,
            gates,
        )
        ends = ()
        if chained:
            parts = tuple(rows // 2 for rows in parts)
            halves = split_parts(
                (halves[0], flip(halves[1], "context", 1)), parts, 2, (pack_projected,)
            )
            ends = (up_halves[1], halves[1])
            input_sent = sent_grad(
                pack_rows, pack_projected, bias_grads, (up_halves[1], halves[1])
            )
            low = add_low(up_halves[0], flip(up_halves[1], "context", 2))
            low = join(low, flip(low, "context", 2), 2, BF)
            grad_up = join(low, flip(low, "context", 1), 1, F32)
            low = add_low(halves[0], flip(halves[1], "context", 2))
            small_parts = tuple(rows // 2 for rows in parts)
            (low,) = join_parts(low, flip(low, "context", 2), small_parts, 2, False)
            grad_down, grad_out, *small, hidden_sum = finish(
                low, flip(low, "context", 1), parts, out_rows, width, up_bias.shape[1]
            )
            received = swapped(input_sent)
            grad_input = product_left(pack_rows[:, :step], pack_projected) + received[
                :step
            ].astype(F32)
            bias_grads = bias_grads.astype(BF).astype(F32) + received[
                step : step + 2, :shard_width
            ].astype(F32)
        else:
            grad_input = scattered(pack_rows, pack_projected, 0)
            bias_grads = lax.psum(bias_grads, "weight")
            grad_down = context_total(scattered(activated, grad_two_low, 1))
            grad_up = context_total(scattered(first_low, grad_pre_low, 0))
            grad_out = context_total(scattered(context, grad_one_low, 1))
            joined = lax.psum(lax.psum(joined, "weight"), "context").reshape(-1)
            small = joined[: 6 * width].reshape(3, 2, width)
            hidden_sum = joined[None, 6 * width : size]
        sent, received = row_total(expand_right(own_block(pack_projected), input_groups), ends)
        total = sent.astype(F32) + received.astype(F32)
        grad_tokens = columns(own_rows(both_halves(grad_one + total)))
        return (
            layer_output,
            grad_tokens,
            grad_input.reshape(1, -1, 3, shard_width),
            bias_grads[None],
            grad_out[None],
            small[0][None],
            small[1][None],
            small[2][None],
            grad_up[None],
            hidden_sum,
            grad_down[None],
        )

    return shards


def solution(mesh):
    token_rows = P(("weight", "context"), None)
    input_spec = P(None, "weight", None, "tensor")
    out_spec = P(None, "tensor", "weight")
    placed = (
        token_rows,
        P(("weight", "context")),
        input_spec,
        P(None, None, "tensor"),
        out_spec,
        P(),
        P(),
        P(),
        P(None, "weight", "tensor"),
        P(None, "tensor"),
        out_spec,
        token_rows,
    )
    return jax.shard_map(
        build(mesh),
        mesh=mesh,
        in_specs=placed,
        out_specs=(
            token_rows,
            token_rows,
            input_spec,
            P(None, None, "tensor"),
            out_spec,
            P(),
            P(),
            P(),
            P(None, "weight", "tensor"),
            P(None, "tensor"),
            out_spec,
        ),
        check_vma=False,
    )
```
